128 devices in a mesh: group: 4 (over z), expert: 32 (over y, x, core).
Axes of the slice: x: 4, y: 4, z: 4, core: 2. Of those that a mesh axis runs over, the one named last changes fastest.
Arguments:
- layer_input: bfloat16 [4096, 4096], P(('group', 'expert')), may hold values from -6 to 6
- out_grad: bfloat16 [4096, 4096], P(('group', 'expert')), may hold values from -6 to 6
- merged: bfloat16 [4096, 4096], P(('group', 'expert')), may hold values from -6 to 6
- head_weight: bfloat16 [4096, 4096], P('group', 'expert'), may hold values from -0.09375 to 0.09375
- merge_weight: bfloat16 [4096, 4096], P('expert', 'group'), may hold values from -0.09375 to 0.09375
- expert_in: bfloat16 [32, 1024, 4096], P('expert', None, 'group'), may hold values from -0.1875 to 0.1875
- expert_out: bfloat16 [32, 4096, 1024], P('expert', 'group'), may hold values from -0.09375 to 0.09375
- dispatched: bfloat16 [32, 1536, 1024], P('expert', 'group'), may hold values from -6 to 6
- expert_ids: int32 [16384, 2], P(('group', 'expert')), may hold values from 0 to 31, all different within a row; in each aligned block of 128 rows (0 to 127, 128 to 255, ...) at most 12 rows name the same one
- gate_values: bfloat16 [16384, 2], P(('group', 'expert')), may hold values from 0.049804688 to 1
Outputs:
- input_grad: bfloat16 [4096, 4096], P(('group', 'expert'))
- head_grad: float32 [4096, 4096], P('group', 'expert')
- merge_grad: float32 [4096, 4096], P('expert', 'group')
- expert_in_grad: float32 [32, 1024, 4096], P('expert', None, 'group')
- expert_out_grad: float32 [32, 4096, 1024], P('expert', 'group')
- gate_grad: bfloat16 [16384, 2], P(('group', 'expert'))
The draws below stay inside these ranges and needn't reach their ends.
Inputs may be any that keep to these rules, and one draw needn't show every extreme that they name: `expert_ids`: each row names two different experts. Within each aligned block of 128 rows (the sub-tokens of one device) no expert is named more than 12 times, and in every draw some block names some expert exactly 12 times.
All inputs are finite; a program needn't handle non-finite values.
Results may differ from the reference program's by a relative error of at most 0.025.
Values may be sent and summed in bfloat16 or wider, within the bound.
A program may use at most 128 MiB of HBM per device.

```python
import math
import jax
import jax.numpy as jnp
import numpy as np
from jax import lax

D = 4096
DS = 1024
FE = 4096
EXPERTS = 32
COLS = 128
TOKENS = 4096
SUB_DEV = 128
SUBS = 16384
SEND = 12
CAP = 384
N_GROUP = 4
N_EXPERT = 32


def shard_levels(rng, dims, shards, smallest, high):
    def one(axis_at, parts):
        steps = jax.random.uniform(jax.random.fold_in(jax.random.fold_in(rng, 6), axis_at), (parts,), jnp.float32, smallest / len(shards), high / len(shards))
        return jnp.repeat(jnp.exp(steps), dims[axis_at] // parts).reshape((-1,) + (1,) * (len(dims) - axis_at - 1))

    loudness = one(*shards[0])
    for cut in shards[1:]:
        loudness = loudness * one(*cut)
    return loudness


def shared_out(key, own, number, rows, amount, top, limit, slope):
    sequence = jax.random.permutation(key, amount)
    crowded, ordinary = shares(amount, rows * top, limit, slope, True), shares(amount, rows * top, limit, slope, False)
    places = jnp.arange(amount)

    def named(sizes, turn):
        used = int((sizes > 0).sum())
        fixed = max(1, used // 4)
        passed = fixed + (places - fixed + turn * (used - fixed)) % max(1, amount - fixed)
        return jnp.zeros((amount,), jnp.int32).at[sequence[jnp.where(places < fixed, places, passed)]].set(jnp.asarray(sizes, jnp.int32))

    sizes = jnp.where(number % 4 == 0, named(crowded, number // 4), named(ordinary, number - number // 4 - 1))
    mixed = jax.random.permutation(jax.random.fold_in(own, 3), amount)
    giver, taker = mixed[0:amount // 2 * 2:2], mixed[1:amount // 2 * 2:2]
    margin = jnp.minimum(sizes[giver] - 1, limit - sizes[taker]) // 2
    margin = jnp.where((giver == sequence[0]) | (taker == sequence[0]) | (sizes[taker] == 0), 0, jnp.maximum(margin, 0))
    passed = jax.random.randint(jax.random.fold_in(own, 4), (amount // 2,), 0, 1 << 20) % (margin + 1)
    sizes = sizes.at[giver].add(-passed).at[taker].add(passed)
    members = jnp.searchsorted(jnp.cumsum(sizes), jnp.arange(rows * top), side="right").astype(jnp.int32)
    grid = members.reshape(top, rows).T
    grid = grid[jax.random.permutation(jax.random.fold_in(own, 1), rows)]
    turn = jax.random.randint(jax.random.fold_in(own, 2), (rows, 1), 0, top)
    return jnp.take_along_axis(grid, (jnp.arange(top)[None, :] + turn) % top, axis=1)


def shares(amount, total, most, slope, full):
    loads = [(1 << 20) // math.isqrt(rank ** slope) + 1 for rank in range(1, amount + 1)]
    largest = most if full else min(most, max(-(-total // amount), total * loads[0] // sum(loads)))
    least = 1 if total - largest >= amount - 1 else 0
    given, spare = [largest] + [least] * (amount - 1), total - largest - least * (amount - 1)
    while spare > 0:
        free = [i for i in range(1, amount) if given[i] < largest] or [i for i in range(1, amount) if given[i] < most]
        pool, left = sum([loads[i] for i in free]), spare
        for i in free:
            extra = min(most - given[i], max(1, left * loads[i] // pool), spare)
            given[i] = given[i] + extra
            spare = spare - extra
    return np.array(given)


def centred(own_key, extent, width, bound, shards=(), kind=jnp.bfloat16):
    values = jax.random.normal(own_key, extent, jnp.float32) * width
    if len(shards) > 0:
        values = shard_levels(own_key, extent, shards, -0.22, 0.18) * values
    return jnp.clip(values, min=-bound, max=bound).astype(kind)


def setup_inputs(seed: int = 0) -> dict:
    key_of = jax.random.split(jax.random.key(seed), 11)
    layer_input = centred(key_of[0], (TOKENS, D), 1.0, 6.0, ((0, 128),))
    out_grad = centred(key_of[1], (TOKENS, D), 1.0, 6.0, ((0, 128),))
    merged = centred(key_of[2], (TOKENS, D), 1.0, 6.0, ((0, 128),))
    head_weight = centred(key_of[3], (D, D), D ** -0.5, 0.09375, ((0, 4), (1, 32)))
    merge_weight = centred(key_of[4], (D, D), D ** -0.5, 0.09375, ((0, 32), (1, 4)))
    expert_in = centred(key_of[5], (EXPERTS, DS, FE), DS ** -0.5, 0.1875, ((0, 32), (2, 4)))
    expert_out = centred(key_of[6], (EXPERTS, FE, DS), FE ** -0.5, 0.09375, ((0, 32), (1, 4)))
    dispatched = centred(key_of[7], (EXPERTS, N_GROUP * CAP, DS), 1.0, 6.0, ((0, 32), (1, 4)))
    expert_ids_keys = jax.random.split(jax.random.fold_in(key_of[8], 1), SUBS // SUB_DEV)
    expert_ids_turns = jax.random.permutation(jax.random.fold_in(key_of[8], 3), SUBS // SUB_DEV)
    expert_ids = jax.vmap(lambda own, number: shared_out(jax.random.fold_in(key_of[8], 2), own, number, SUB_DEV, EXPERTS, 2, SEND, 2))(expert_ids_keys, expert_ids_turns).reshape((SUBS, 2))
    gate_values = jnp.clip(0.049804688 + 0.9501953 * jax.random.uniform(key_of[9], (SUBS, 2), jnp.float32) ** shard_levels(key_of[9], (SUBS, 2), ((0, 128),), -0.2, 0.2), 0.049804688, 1.0).astype(jnp.bfloat16)
    return dict(layer_input=layer_input, out_grad=out_grad, merged=merged, head_weight=head_weight, merge_weight=merge_weight, expert_in=expert_in, expert_out=expert_out, dispatched=dispatched, expert_ids=expert_ids, gate_values=gate_values)


root_scale = 0.7978845608028654
cubic_term = 0.044715


def gelu_value(value):
    inner = root_scale * (value + cubic_term * value * value * value)
    return 0.5 * value * (1.0 + jnp.tanh(inner))


def gelu_slope(value):
    inner = root_scale * (value + cubic_term * value * value * value)
    tangent = jnp.tanh(inner)
    return 0.5 * (1.0 + tangent) + 0.5 * value * (1.0 - tangent * tangent) * root_scale * (1.0 + 3.0 * cubic_term * value * value)


def slot_rows(expert_ids):
    blocks = expert_ids.reshape(-1, 2 * SUB_DEV)
    onehot = (blocks[:, :, None] == jnp.arange(EXPERTS, dtype=jnp.int32)[None, None, :]).astype(jnp.int32)
    running = jnp.cumsum(onehot, axis=1)
    slots = jnp.sum(onehot * running, axis=2) - 1
    block_index = jnp.arange(blocks.shape[0], dtype=jnp.int32)[:, None]
    return (block_index * SEND + slots).reshape(-1).astype(jnp.int32)


def reference(layer_input, out_grad, merged, head_weight, merge_weight, expert_in, expert_out, dispatched, expert_ids, gate_values):
    merged_grad = jnp.dot(out_grad, merge_weight.T, preferred_element_type=jnp.float32).astype(jnp.bfloat16)
    merge_grad = jnp.dot(merged.T, out_grad, preferred_element_type=jnp.float32)
    sub_grad = merged_grad.reshape(SUBS, DS)
    flat_ids = expert_ids.reshape(-1).astype(jnp.int32)
    flat_rows = slot_rows(expert_ids)
    repeated = jnp.repeat(sub_grad, 2, axis=0)
    flat_gates = gate_values.reshape(-1)
    buffer_rows = N_GROUP * CAP
    comb_buffer = jnp.zeros((EXPERTS, buffer_rows, DS), jnp.bfloat16).at[flat_ids, flat_rows].set(repeated)
    gate_buffer = jnp.zeros((EXPERTS, buffer_rows), jnp.bfloat16).at[flat_ids, flat_rows].set(flat_gates)

    def one_expert(operands):
        combined, gates, inputs, weight_in, weight_out = operands
        before = jnp.dot(inputs, weight_in, preferred_element_type=jnp.float32)
        hidden = gelu_value(before).astype(jnp.bfloat16)
        produced = jnp.dot(hidden, weight_out, preferred_element_type=jnp.float32)
        scaled = (gates.astype(jnp.float32)[:, None] * combined.astype(jnp.float32)).astype(jnp.bfloat16)
        hidden_grad = jnp.dot(scaled, weight_out.T, preferred_element_type=jnp.float32)
        before_grad = (hidden_grad * gelu_slope(before)).astype(jnp.bfloat16)
        out_weight_grad = jnp.dot(hidden.T, scaled, preferred_element_type=jnp.float32)
        in_weight_grad = jnp.dot(inputs.T, before_grad, preferred_element_type=jnp.float32)
        row_grad = jnp.dot(before_grad, weight_in.T, preferred_element_type=jnp.float32).astype(jnp.bfloat16)
        slot_gate = jnp.sum(combined.astype(jnp.float32) * produced, axis=1).astype(jnp.bfloat16)
        return in_weight_grad, out_weight_grad, row_grad, slot_gate

    expert_in_grad, expert_out_grad, row_grad, slot_gate = lax.map(one_expert, (comb_buffer, gate_buffer, dispatched, expert_in, expert_out))
    picked = row_grad[flat_ids, flat_rows].astype(jnp.float32).reshape(SUBS, 2, DS)
    head_out_grad = jnp.sum(gate_values.astype(jnp.float32)[:, :, None] * picked, axis=1).astype(jnp.bfloat16).reshape(TOKENS, D)
    gate_grad = slot_gate[flat_ids, flat_rows].reshape(SUBS, 2)
    head_grad = jnp.dot(layer_input.T, head_out_grad, preferred_element_type=jnp.float32)

    def add_block(total, index):
        columns = lax.dynamic_slice_in_dim(head_out_grad, index * COLS, COLS, 1)
        weights = lax.dynamic_slice_in_dim(head_weight, index * COLS, COLS, 1)
        term = jnp.dot(columns, weights.T, preferred_element_type=jnp.float32).astype(jnp.bfloat16)
        term = lax.optimization_barrier(term)
        return total + term.astype(jnp.float32), index

    total, leftover = lax.scan(add_block, jnp.zeros((TOKENS, D), jnp.float32), jnp.arange(N_EXPERT, dtype=jnp.int32))
    input_grad = total.astype(jnp.bfloat16)
    return input_grad, head_grad, merge_grad, expert_in_grad, expert_out_grad, gate_grad
```

```python
import jax
import jax.numpy as jnp
from jax import lax
from jax.experimental import pallas as pl
from jax.experimental.pallas import tpu as pltpu
from jax.sharding import PartitionSpec as P

MESH = pl.DeviceIdType.MESH
BF = jnp.bfloat16
F32 = jnp.float32
MIB = 1 << 20

root_scale = 0.7978845608028654
cubic_term = 0.044715


def gelu_pair(value):
    square = value * value
    tangent = jnp.tanh(root_scale * value * (1.0 + cubic_term * square))
    half = 0.5 * (1.0 + tangent)
    slope = half + 0.5 * value * (1.0 - tangent * tangent) * root_scale * (
        1.0 + 3.0 * cubic_term * square
    )
    return value * half, slope


def dot(left, right, dims):
    return lax.dot_general(left, right, ((dims[:1], dims[1:]), ((), ())), preferred_element_type=F32)


NN, NT, TN = (1, 0), (1, 1), (0, 0)


def wrap(value):
    return lax.rem(value + 8, 4)


def place():
    e = lax.axis_index("expert")
    return lax.axis_index("group"), lax.rem(lax.div(e, 2), 4), lax.div(e, 8), lax.rem(e, 2)


def at(z, x, y, c):
    return {"group": z, "expert": (y * 4 + x) * 2 + c}


def by_chip(z, chip, c):
    return {"group": z, "expert": chip * 2 + c}


def rows(start, size):
    return pl.ds(pl.multiple_of(start, 16), size)


def lanes(start, size):
    return pl.ds(pl.multiple_of(start, 128), size)


def send(src, dst, ss, rs, device):
    pltpu.make_async_remote_copy(
        src_ref=src, dst_ref=dst, send_sem=ss, recv_sem=rs, device_id=device, device_id_type=MESH
    ).start()


def wait(ref, sem):
    pltpu.make_async_copy(ref, ref, sem).wait()


class PlaneGather:
    def __init__(self, buf, ss, rs, me):
        self.buf, self.ss, self.rs, self.me = buf, ss, rs, me
        self.sent = []

    def shift(self, h, i, j):
        z, x, y, c = self.me
        dx, dy = (i, j) if h == 0 else (j, i)
        return wrap(x + dx), wrap(y + dy)

    def piece(self, h, spot, half=None):
        px, py = self.shift(h, *spot)
        row = h * 512 + (py * 4 + px) * 32
        if half is None:
            return self.buf.at[rows(row, 32)]
        return self.buf.at[rows(row + 16 * half, 16)]

    def spot(self, stage, i, j):
        return (j, 0) if stage == 0 else (i, j)

    def sem(self, h, stage, i, kind):
        return h * 20 + (0 if stage == 0 else 4 + 4 * (i % 4)) + kind

    def go(self, ref, h, stage, i, kind, step):
        s = self.sem(h, stage, i, kind)
        px, py = self.shift(h, *((step, 0) if stage == 0 else (0, step)))
        send(ref, ref, self.ss.at[s], self.rs.at[s], at(self.me[0], px, py, self.me[3]))
        self.sent.append((ref, s))

    def begin(self, h, stage, i=0):
        ref = self.piece(h, self.spot(stage, i, 0))
        self.go(ref, h, stage, i, 0, 1)
        self.go(ref, h, stage, i, 1, -1)

    def take(self, h, stage, i, kind):
        spot = self.spot(stage, i, (-1, 1)[kind])
        wait(self.piece(h, spot), self.rs.at[self.sem(h, stage, i, kind)])
        self.go(self.piece(h, spot, kind), h, stage, i, kind + 2, (1, -1)[kind])

    def relay(self, h, stage, i=0):
        self.take(h, stage, i, 0)
        self.take(h, stage, i, 1)

    def finish(self, h, stage, i=0):
        for kind in (2, 3):
            ref = self.piece(h, self.spot(stage, i, 2), kind - 2)
            wait(ref, self.rs.at[self.sem(h, stage, i, kind)])

    def first(self, h):
        self.begin(h, 0)
        self.begin(h, 1, 0)

    def steps(self):
        for h in (0, 1):
            self.take(h, 0, 0, 0)
            self.begin(h, 1, -1)
            self.take(h, 0, 0, 1)
            self.begin(h, 1, 1)
        yield
        for h in (0, 1):
            self.relay(h, 1, 0)
        for h in (0, 1):
            self.finish(h, 0)
            self.begin(h, 1, 2)
        yield
        for i in (-1, 1):
            for h in (0, 1):
                self.relay(h, 1, i)
            yield
        for h in (0, 1):
            self.relay(h, 1, 2)
        yield
        for i in (0, -1, 1, 2):
            for h in (0, 1):
                self.finish(h, 1, i)
        yield
        for ref, s in self.sent:
            wait(ref, self.ss.at[s])


class PlaneScatter(PlaneGather):
    def __init__(self, buf, halves, wholes, ss, rs, me):
        super().__init__(buf, ss, rs, me)
        self.halves, self.wholes = halves, wholes

    def ring(self, h, stage, i):
        return h * 5 + (0 if stage == 0 else 1 + i % 4)

    def post(self, ref, dst, h, stage, i, kind, step):
        s = self.sem(h, stage, i, kind)
        px, py = self.shift(h, *((step, 0) if stage == 0 else (0, step)))
        send(ref, dst, self.ss.at[s], self.rs.at[s], at(self.me[0], px, py, self.me[3]))
        self.sent.append((ref, s))

    def open(self, h, stage, i=0):
        r = self.ring(h, stage, i)
        for kind, step in ((0, 1), (1, -1)):
            ref = self.piece(h, self.spot(stage, i, 2), kind)
            self.post(ref, self.halves.at[r, kind], h, stage, i, kind, step)

    def middle(self, h, stage, i=0):
        r = self.ring(h, stage, i)
        for kind, step in ((0, 1), (1, -1)):
            got = self.halves.at[r, kind]
            wait(got, self.rs.at[self.sem(h, stage, i, kind)])
            own = self.piece(h, self.spot(stage, i, step), kind)
            own[...] = (own[...].astype(F32) + got[...].astype(F32)).astype(BF)
            ref = self.piece(h, self.spot(stage, i, step))
            self.post(ref, self.wholes.at[r, kind], h, stage, i, kind + 2, step)

    def close(self, h, stage, i=0):
        r = self.ring(h, stage, i)
        for kind in (0, 1):
            wait(self.wholes.at[r, kind], self.rs.at[self.sem(h, stage, i, kind + 2)])
        own = self.piece(h, self.spot(stage, i, 0))
        own[...] = (
            own[...].astype(F32)
            + self.wholes[r, 0].astype(F32)
            + self.wholes[r, 1].astype(F32)
        ).astype(BF)

    def run(self):
        for i in (2, -1, 1, 0):
            for h in (0, 1):
                self.open(h, 1, i)
        for i in (2, -1, 1, 0):
            for h in (0, 1):
                self.middle(h, 1, i)
        for h in (0, 1):
            self.close(h, 1, 2)
            self.open(h, 0)
        for i in (-1, 1):
            for h in (0, 1):
                self.close(h, 1, i)
        for h in (0, 1):
            self.middle(h, 0)
        for h in (0, 1):
            self.close(h, 1, 0)
        for h in (0, 1):
            self.close(h, 0)

    def done(self):
        for ref, s in self.sent:
            wait(ref, self.ss.at[s])


class Fourfold:
    def __init__(self, src, slot, ss, rs, me):
        self.src, self.slot, self.ss, self.rs, self.me = src, slot, ss, rs, me
        z, x, y, c = me
        self.core = lax.div(z, 2)
        self.own = self.core == c

    def start(self):
        z, x, y, c = self.me
        dst = self.slot(lax.rem(z, 2), c)
        r = lax.rem(z, 2) * 2 + c

        @pl.when(self.own)
        def _():
            pltpu.make_async_copy(self.src, dst, self.rs.at[r]).start()

        @pl.when(jnp.logical_not(self.own))
        def _():
            send(self.src, dst, self.ss.at[0], self.rs.at[r], at(z, x, y, self.core))

        for k in (1, 3, 2):
            send(self.src, dst, self.ss.at[k], self.rs.at[r], at(wrap(z + k), x, y, self.core))

    def arrive(self):
        for i in (0, 1):
            for j in (0, 1):
                wait(self.slot(i, j), self.rs.at[i * 2 + j])

    def done(self):
        @pl.when(jnp.logical_not(self.own))
        def _():
            wait(self.src, self.ss.at[0])

        for k in (1, 2, 3):
            wait(self.src, self.ss.at[k])


class Fold:
    def __init__(self, out, got, ss, rs, me):
        self.out, self.got, self.ss, self.rs, self.me = out, got, ss, rs, me

    def start(self, i, j):
        z, x, y, c = self.me
        p = i * 2 + j
        to = 2 * c + i
        own = jnp.logical_and(to == z, c == j)

        @pl.when(own)
        def _():
            pltpu.make_async_copy(self.out.at[p], self.got.at[z], self.rs.at[z]).start()

        @pl.when(jnp.logical_not(own))
        def _():
            send(self.out.at[p], self.got.at[z], self.ss.at[p], self.rs.at[z], at(to, x, y, j))

    def arrive(self):
        for i in range(4):
            wait(self.got.at[i], self.rs.at[i])

    def done(self):
        z, x, y, c = self.me
        for i in (0, 1):
            for j in (0, 1):
                own = jnp.logical_and(2 * c + i == z, c == j)

                @pl.when(jnp.logical_not(own))
                def _():
                    wait(self.out.at[i * 2 + j], self.ss.at[i * 2 + j])


class ChipSwap:
    def __init__(self, src, dst, ss, rs, me):
        self.src, self.dst, self.ss, self.rs, self.me = src, dst, ss, rs, me
        self.chip = me[2] * 4 + me[1]

    def start(self):
        z, x, y, c = self.me
        mine = self.chip

        def step(k, _):
            to = lax.rem(mine + k, 16)
            send(self.src(to), self.dst(mine), self.ss.at[k], self.rs.at[k], by_chip(z, to, c))
            return 0

        pltpu.make_async_copy(self.src(mine), self.dst(mine), self.rs.at[0]).start()
        lax.fori_loop(1, 16, step, 0)

    def arrive(self):
        def step(k, _):
            wait(self.dst(lax.rem(self.chip + 16 - k, 16)), self.rs.at[k])
            return 0

        lax.fori_loop(0, 16, step, 0)

    def done(self):
        def step(k, _):
            wait(self.src(lax.rem(self.chip + k, 16)), self.ss.at[k])
            return 0

        lax.fori_loop(1, 16, step, 0)


class DeviceSwap:
    def __init__(self, out, got, ss, rs, z):
        self.out, self.got, self.ss, self.rs, self.z = out, got, ss, rs, z
        self.e = lax.axis_index("expert")

    def start(self):
        mine = self.e

        def step(k, _):
            to = lax.rem(mine + k, 32)
            send(
                self.out.at[rows(16 * to, 16)],
                self.got.at[rows(16 * mine, 16)],
                self.ss.at[k],
                self.rs.at[k],
                {"group": self.z, "expert": to},
            )
            return 0

        pltpu.make_async_copy(
            self.out.at[rows(16 * mine, 16)], self.got.at[rows(16 * mine, 16)], self.rs.at[0]
        ).start()
        lax.fori_loop(1, 32, step, 0)

    def arrive(self):
        def step(k, _):
            wait(self.got.at[rows(16 * lax.rem(self.e + 32 - k, 32), 16)], self.rs.at[k])
            return 0

        lax.fori_loop(0, 32, step, 0)

    def done(self):
        def step(k, _):
            wait(self.out.at[rows(16 * lax.rem(self.e + k, 32), 16)], self.ss.at[k])
            return 0

        lax.fori_loop(1, 32, step, 0)


class DepthGather:
    def __init__(self, src, buf, ss, rs, me):
        self.src, self.buf, self.ss, self.rs, self.me = src, buf, ss, rs, me

    def piece(self, step, half=None):
        row = 384 * wrap(self.me[0] + step)
        if half is None:
            return self.buf.at[rows(row, 384)]
        return self.buf.at[rows(row + 192 * half, 192)]

    def to(self, step):
        z, x, y, c = self.me
        return at(wrap(z + step), x, y, c)

    def start(self):
        dst = self.piece(0)
        send(self.src, dst, self.ss.at[0], self.rs.at[0], self.to(1))
        send(self.src, dst, self.ss.at[1], self.rs.at[1], self.to(-1))

    def take(self, kind):
        step = (-1, 1)[kind]
        wait(self.piece(step), self.rs.at[kind])
        half = self.piece(step, kind)
        send(half, half, self.ss.at[2 + kind], self.rs.at[2 + kind], self.to(-step))

    def finish(self, kind):
        wait(self.piece(2, kind), self.rs.at[2 + kind])

    def done(self):
        for kind in (0, 1):
            wait(self.src, self.ss.at[kind])
            wait(self.piece((-1, 1)[kind], kind), self.ss.at[2 + kind])


def dma(*shape):
    return pltpu.SemaphoreType.DMA(shape)


def merge_kernel(og, mw, merged, disp, tg, mgo, xin, buf, mwb, mc, sib_out, sib_in, tgc,
                 gs, gr, ws, wr, cs, cr, ts, tr, zs, zr, ls, bs, br):
    me = place()
    z, x, y, c = me
    chip = y * 4 + x
    other = at(z, x, y, 1 - c)
    mine = buf.at[rows(c * 512 + chip * 32, 32)]
    theirs = buf.at[rows((1 - c) * 512 + chip * 32, 32)]
    send(og.at[:, lanes((1 - c) * 2048, 2048)], mine, bs.at[0], br.at[0], other)
    local = pltpu.make_async_copy(og.at[:, lanes(c * 2048, 2048)], mine, ls.at[0])
    local.start()
    weights = Fourfold(
        mw, lambda i, j: mwb.at[rows(128 * j, 128), lanes(1024 * i, 1024)], ws, wr, me
    )
    weights.start()
    columns = ChipSwap(
        lambda to: merged.at[:, lanes(256 * to, 256)],
        lambda k: mc.at[rows(c * 512 + k * 32, 32)],
        cs, cr, me,
    )
    local.wait()
    wait(theirs, br.at[0])
    gather = PlaneGather(buf, gs, gr, me)
    for h in (0, 1):
        gather.first(h)
    columns.start()
    depth = DepthGather(disp, xin, zs, zr, me)
    depth.start()
    keep = pltpu.make_async_copy(disp, xin.at[rows(384 * z, 384)], ls.at[1])
    keep.start()
    for _ in gather.steps():
        pass
    weights.arrive()

    def product(h, tile):
        return dot(buf[rows(h * 512 + tile * 256, 256), :], mwb[...], NT)

    for tile in (0, 1):
        sib_out[pl.ds(tile * 256, 256), :] = product(1 - c, tile).astype(BF)
    send(sib_out, sib_in, bs.at[1], br.at[1], other)
    columns.arrive()
    half = mc.at[rows(c * 512, 512)]
    send(half, half, bs.at[2], br.at[2], other)
    own = [product(c, tile) for tile in (0, 1)]
    wait(sib_in, br.at[1])
    for tile in (0, 1):
        part = pl.ds(tile * 256, 256)
        tgc[part, :] = (own[tile] + sib_in[part, :].astype(F32)).astype(BF)
    tokens = ChipSwap(
        lambda to: tgc.at[rows(32 * to, 32)],
        lambda k: tg.at[:, lanes(256 * k, 256)],
        ts, tr, me,
    )
    tokens.start()
    depth.take(0)
    depth.take(1)
    wait(mc.at[rows((1 - c) * 512, 512)], br.at[2])
    for tile in range(4):
        sums = dot(mc[...], buf[:, tile * 512:tile * 512 + 512], TN).astype(BF)
        for j in (0, 1):
            mgo[(tile // 2) * 2 + j, :, (tile % 2) * 512:(tile % 2) * 512 + 512] = sums[
                128 * j:128 * j + 128
            ]
    tokens.arrive()
    depth.finish(0)
    depth.finish(1)
    keep.wait()
    weights.done()
    columns.done()
    tokens.done()
    depth.done()
    wait(mine, bs.at[0])
    wait(sib_out, bs.at[1])
    wait(half, bs.at[2])


def expert_kernel(tg, pg, sel, sums, mask, last, xin, w_in, w_out, li, hw,
                  hog, ing, outg, retg, lih, hwh,
                  outb, inb, sc, xv, wi, wo, hid, slope, bg, rp, fb, wb, sgo, sgi, back, ret,
                  s1, r1, s2, r2, gs, gr, hs, hr, zs, zr, fs, fr, qs, qr, ls, bs, br):
    me = place()
    z, x, y, c = me
    chip = y * 4 + x
    other = at(z, x, y, 1 - c)
    loads = [
        pltpu.make_async_copy(src, dst, ls.at[k])
        for k, (src, dst) in enumerate(((w_in, wi), (xin, xv), (w_out, wo)))
    ]
    for load in loads:
        load.start()
    for part in range(2):
        total = jnp.zeros((512, 512), F32)
        for h in range(4):
            first = h * 1024 + part * 512
            total = total + dot(pg[h], tg[:, first:first + 512], NN)
        outb[:, part * 512:part * 512 + 512] = total.astype(BF)
    there = DeviceSwap(outb, inb, s1, r1, z)
    there.start()
    head = Fourfold(
        hw, lambda i, j: hwh.at[rows(1024 * i, 1024), lanes(128 * j, 128)], hs, hr, me
    )
    head.start()
    mine = lih.at[rows(c * 512 + chip * 32, 32)]
    theirs = lih.at[rows((1 - c) * 512 + chip * 32, 32)]
    send(li.at[:, lanes((1 - c) * 2048, 2048)], mine, bs.at[0], br.at[0], other)
    keep = pltpu.make_async_copy(li.at[:, lanes(c * 2048, 2048)], mine, ls.at[3])
    keep.start()
    loads[0].wait()
    loads[1].wait()

    def early(t, _):
        part = rows(128 * t, 128)
        value, grade = gelu_pair(dot(xv[part, :], wi[...], NN))
        hid[part, :] = value.astype(BF)
        slope[part, :] = grade
        return 0

    lax.fori_loop(0, 12, early, 0)
    keep.wait()
    wait(theirs, br.at[0])
    there.arrive()
    own_rows = rows(384 * z, 384)
    sc[own_rows, :] = dot(sel[...], inb[...], NN).astype(BF)
    depth = DepthGather(sc.at[own_rows], sc, zs, zr, me)
    depth.start()
    gather = PlaneGather(lih, gs, gr, me)
    for h in (0, 1):
        gather.first(h)
    progress = gather.steps()
    loads[2].wait()

    def chunk(step):
        q = wrap(z + step)
        part = rows(384 * q, 384)
        grad = dot(sc[part, :], wo[...], NT)
        column = jnp.sum(grad * hid[part, :].astype(F32), axis=1, keepdims=True)
        sgo[q] = dot(sums[...], (column * mask[...]).astype(BF), NN).astype(BF)
        bg[part, :] = (grad * slope[part, :]).astype(BF)
        rp[part, :] = dot(bg[part, :], wi[...], NT).astype(BF)
        if step:
            send(sgo.at[q], sgi.at[z], qs.at[step], qr.at[4 - step], at(q, x, y, c))

    chunk(0)
    next(progress)
    depth.take(0)
    depth.take(1)
    next(progress)
    chunk(1)
    chunk(3)
    next(progress)
    depth.finish(0)
    depth.finish(1)
    chunk(2)

    def rowpart(step, half=None):
        row = 384 * wrap(z + step)
        if half is None:
            return rp.at[rows(row, 384)]
        return rp.at[rows(row + 192 * half, 192)]

    for kind, step in ((0, 1), (1, -1)):
        send(rowpart(2, kind), fb.at[kind], fs.at[kind], fr.at[kind], at(wrap(z + step), x, y, c))
    next(progress)
    for kind, step in ((0, 1), (1, -1)):
        wait(fb.at[kind], fr.at[kind])
        target = rowpart(step, kind)
        target[...] = (target[...].astype(F32) + fb[kind].astype(F32)).astype(BF)
        send(rowpart(step), wb.at[kind], fs.at[2 + kind], fr.at[2 + kind],
             at(wrap(z + step), x, y, c))
    next(progress)

    def weight(t, _):
        part = lanes(256 * t, 256)
        ing[:, part] = dot(xv[...], bg[:, part], TN)
        outg[:, part] = dot(hid[...], sc[:, part], TN)
        return 0

    lax.fori_loop(0, 4, weight, 0)
    for step in (1, 2, 3):
        wait(sgi.at[wrap(z + step)], qr.at[step])
    marks = sgo[z].astype(F32)
    for step in (1, 2, 3):
        marks = marks + sgi[wrap(z + step)].astype(F32)
    for kind in (0, 1):
        wait(wb.at[kind], fr.at[2 + kind])
    total = (rp[own_rows, :].astype(F32) + wb[0].astype(F32) + wb[1].astype(F32)).astype(BF)
    back[...] = dot(sel[...], total, TN).astype(BF)
    spread = dot(last[...], marks.astype(BF), NN)
    back[:, 0:128] = (back[:, 0:128].astype(F32) + spread).astype(BF)
    home = DeviceSwap(back, ret, s2, r2, z)
    home.start()
    for _ in progress:
        pass
    head.arrive()
    home.arrive()
    for h in range(4):
        hog[:, h * 1024:h * 1024 + 1024] = dot(pg[h], ret[...], TN).astype(BF)
    retg[...] = ret[:, 0:128]
    there.done()
    home.done()
    head.done()
    depth.done()
    wait(mine, bs.at[0])
    for step in (1, 2, 3):
        wait(sgo.at[wrap(z + step)], qs.at[step])
    for kind in (0, 1):
        wait(rowpart(2, kind), fs.at[kind])
        wait(rowpart((1, -1)[kind]), fs.at[2 + kind])


def head_kernel(hog, lih, hwh, mgo, ig, hg, mg,
                hc, part, liv, hwv, halves, wholes, hgo, hgi, mgi,
                cs, cr, gs, gr, hs, hr, ms, mr, ls, bs, br):
    me = place()
    z, x, y, c = me
    chip = y * 4 + x
    other = at(z, x, y, 1 - c)
    columns = ChipSwap(
        lambda to: hog.at[:, lanes(256 * to, 256)],
        lambda k: hc.at[rows(c * 512 + k * 32, 32)],
        cs, cr, me,
    )
    columns.start()
    loads = [
        pltpu.make_async_copy(src, dst, ls.at[k])
        for k, (src, dst) in enumerate(((hwh, hwv), (lih, liv)))
    ]
    for load in loads:
        load.start()
    merge = Fold(mgo, mgi, ms, mr, me)
    for i in (0, 1):
        for j in (0, 1):
            merge.start(i, j)
    columns.arrive()
    half = hc.at[rows(c * 512, 512)]
    send(half, half, bs.at[0], br.at[0], other)
    loads[0].wait()

    def product(h):
        def step(t, _):
            tile = rows(h * 512 + 128 * t, 128)
            part[tile, :] = dot(hc[tile, :], hwv[...], NT).astype(BF)
            return 0

        lax.fori_loop(0, 4, step, 0)

    product(c)
    wait(hc.at[rows((1 - c) * 512, 512)], br.at[0])
    product(1 - c)
    scatter = PlaneScatter(part, halves, wholes, gs, gr, me)
    loads[1].wait()
    head = Fold(hgo, hgi, hs, hr, me)
    scatter.run()
    for i in (0, 1):
        for tile in (0, 1):
            sums = dot(liv[:, i * 1024 + tile * 512:i * 1024 + tile * 512 + 512], hc[...], TN)
            for j in (0, 1):
                hgo[i * 2 + j, tile * 512:tile * 512 + 512, :] = sums[
                    :, 128 * j:128 * j + 128
                ].astype(BF)
        for j in (0, 1):
            head.start(i, j)
    give = part.at[rows((1 - c) * 512 + chip * 32, 32)]
    mine = part.at[rows(c * 512 + chip * 32, 32)]
    seen = ig.at[:, lanes((1 - c) * 2048, 2048)]
    there = ig.at[:, lanes(c * 2048, 2048)]
    send(give, there, bs.at[1], br.at[1], other)
    keep = pltpu.make_async_copy(mine, there, ls.at[2])
    keep.start()
    merge.arrive()
    mg[...] = (mgi[0].astype(F32) + mgi[1].astype(F32)) + (mgi[2].astype(F32) + mgi[3].astype(F32))
    head.arrive()
    hg[...] = (hgi[0].astype(F32) + hgi[1].astype(F32)) + (hgi[2].astype(F32) + hgi[3].astype(F32))
    wait(seen, br.at[1])
    keep.wait()
    scatter.done()
    columns.done()
    merge.done()
    head.done()
    wait(half, bs.at[0])
    wait(give, bs.at[1])


VM = pl.BlockSpec(memory_space=pltpu.VMEM)
ANY = pl.BlockSpec(memory_space=pl.ANY)


def call(kernel, operands, specs, outs, out_specs, scratch, limit, flops):
    return pl.pallas_call(
        kernel,
        out_shape=[jax.ShapeDtypeStruct(shape, kind) for shape, kind in outs],
        in_specs=specs,
        out_specs=out_specs,
        scratch_shapes=[pltpu.VMEM(s[0], s[1]) if isinstance(s, tuple) else s for s in scratch],
        compiler_params=pltpu.CompilerParams(
            has_side_effects=True, vmem_limit_bytes=limit * MIB
        ),
        cost_estimate=pl.CostEstimate(flops=flops, bytes_accessed=1 << 24, transcendentals=0),
    )(*operands)


def body(
    layer_input, out_grad, merged, head_weight, merge_weight,
    expert_in, expert_out, dispatched, expert_ids, gate_values,
):
    flat_ids = expert_ids.reshape(-1)
    onehot = (flat_ids[:, None] == jnp.arange(32, dtype=jnp.int32)[None, :]).astype(jnp.int32)
    ranks = jnp.sum(onehot * jnp.cumsum(onehot, axis=0), axis=1) - 1
    targets = (flat_ids * 16 + ranks).reshape(32, 4, 2).transpose(1, 0, 2)
    gates = gate_values.astype(F32).reshape(32, 4, 2).transpose(1, 0, 2)
    slots = jnp.arange(512, dtype=jnp.int32)[None, :, None]
    pg = (
        jnp.where(slots == targets[:, None, :, 0], gates[:, None, :, 0], 0.0)
        + jnp.where(slots == targets[:, None, :, 1], gates[:, None, :, 1], 0.0)
    ).astype(BF)
    row = jnp.arange(384, dtype=jnp.int32)[:, None]
    sel = ((row // 12) * 16 + row % 12 == jnp.arange(512, dtype=jnp.int32)[None, :]).astype(BF)
    sums = (jnp.arange(32, dtype=jnp.int32)[:, None] == (row // 12).reshape(1, 384)).astype(BF)
    mask = (row % 12 == jnp.arange(128, dtype=jnp.int32)[None, :]).astype(F32)
    last = (
        jnp.arange(512, dtype=jnp.int32)[:, None]
        == jnp.arange(32, dtype=jnp.int32)[None, :] * 16 + 12
    ).astype(BF)

    tg, mgo, xin = call(
        merge_kernel,
        (out_grad, merge_weight, merged, dispatched[0]),
        [ANY] * 4,
        [((32, 4096), BF), ((4, 128, 1024), BF), ((1536, 1024), BF)],
        [VM, VM, ANY],
        [
            ((1024, 2048), BF), ((256, 2048), BF), ((1024, 256), BF),
            ((512, 256), BF), ((512, 256), BF), ((512, 256), BF),
            dma(40), dma(40), dma(4), dma(4), dma(16), dma(16), dma(16), dma(16),
            dma(4), dma(4), dma(2), dma(3), dma(3),
        ],
        32, 1 << 31,
    )
    hog, in_grad, out_weight_grad, retg, lih, hwh = call(
        expert_kernel,
        (tg, pg, sel, sums, mask, last, xin, expert_in[0], expert_out[0], layer_input, head_weight),
        [VM] * 6 + [ANY] * 5,
        [
            ((32, 4096), BF), ((1024, 1024), F32), ((1024, 1024), F32), ((512, 128), BF),
            ((1024, 2048), BF), ((2048, 256), BF),
        ],
        [VM, VM, VM, VM, ANY, ANY],
        [
            ((512, 1024), BF), ((512, 1024), BF), ((1536, 1024), BF), ((1536, 1024), BF),
            ((1024, 1024), BF), ((1024, 1024), BF), ((1536, 1024), BF), ((1536, 1024), F32),
            ((1536, 1024), BF), ((1536, 1024), BF), ((2, 192, 1024), BF), ((2, 384, 1024), BF),
            ((4, 32, 128), BF), ((4, 32, 128), BF), ((512, 1024), BF), ((512, 1024), BF),
            dma(32), dma(32), dma(32), dma(32), dma(40), dma(40), dma(4), dma(4),
            dma(4), dma(4), dma(4), dma(4), dma(4), dma(4), dma(4), dma(1), dma(1),
        ],
        56, 1 << 34,
    )
    input_total, head_grad, merge_grad = call(
        head_kernel,
        (hog, lih, hwh, mgo),
        [VM, ANY, ANY, VM],
        [((32, 4096), BF), ((1024, 128), F32), ((128, 1024), F32)],
        [VM, VM, VM],
        [
            ((1024, 256), BF), ((1024, 2048), BF), ((1024, 2048), BF), ((2048, 256), BF),
            ((10, 2, 16, 2048), BF), ((10, 2, 32, 2048), BF),
            ((4, 1024, 128), BF), ((4, 1024, 128), BF), ((4, 128, 1024), BF),
            dma(16), dma(16), dma(40), dma(40), dma(4), dma(4), dma(4), dma(4),
            dma(3), dma(2), dma(2),
        ],
        40, 1 << 31,
    )
    found = jnp.dot(
        onehot.astype(BF), retg.reshape(32, 16, 128)[:, 12, :], preferred_element_type=F32
    )
    spot = ranks[:, None] == jnp.arange(128, dtype=jnp.int32)[None, :]
    gate_grad = (
        jnp.sum(jnp.where(spot, found, 0.0), axis=1).reshape(128, 2) / gate_values.astype(F32)
    ).astype(BF)
    return (input_total, head_grad, merge_grad, in_grad[None], out_weight_grad[None], gate_grad)


def solution(mesh):
    placed = (
        P(("group", "expert"), None),
        P(("group", "expert"), None),
        P(("group", "expert"), None),
        P("group", "expert"),
        P("expert", "group"),
        P("expert", None, "group"),
        P("expert", "group", None),
        P("expert", "group", None),
        P(("group", "expert"), None),
        P(("group", "expert"), None),
    )
    return jax.shard_map(
        body,
        mesh=mesh,
        in_specs=placed,
        out_specs=(
            P(("group", "expert"), None),
            P("group", "expert"),
            P("expert", "group"),
            P("expert", None, "group"),
            P("expert", "group", None),
            P(("group", "expert"), None),
        ),
        check_vma=False,
    )
```

```python
import jax
import jax.numpy as jnp
from jax import lax
from jax.experimental import pallas as pl
from jax.experimental.pallas import tpu as pltpu
from jax.sharding import PartitionSpec as P

MESH = pl.DeviceIdType.MESH
BF = jnp.bfloat16
F32 = jnp.float32
LIMIT = 63 << 20

root_scale = 0.7978845608028654
cubic_term = 0.044715


def gelu_pair(value):
    square = value * value
    tangent = jnp.tanh(root_scale * value * (1.0 + cubic_term * square))
    half = 0.5 * (1.0 + tangent)
    slope = half + 0.5 * value * (1.0 - tangent * tangent) * root_scale * (
        1.0 + 3.0 * cubic_term * square
    )
    return value * half, slope


def dot(left, right, dims):
    return lax.dot_general(left, right, ((dims[:1], dims[1:]), ((), ())), preferred_element_type=F32)


NN, NT, TN = (1, 0), (1, 1), (0, 0)


def wrap(value):
    return lax.rem(value + 8, 4)


def place():
    e = lax.axis_index("expert")
    return lax.axis_index("group"), lax.rem(lax.div(e, 2), 4), lax.div(e, 8), lax.rem(e, 2)


def at(z, x, y, c):
    return {"group": z, "expert": (y * 4 + x) * 2 + c}


def by_chip(z, chip, c):
    return {"group": z, "expert": chip * 2 + c}


def rows(start, size):
    return pl.ds(pl.multiple_of(start, 16), size)


def lanes(start, size):
    return pl.ds(pl.multiple_of(start, 128), size)


def send(src, dst, ss, rs, device):
    pltpu.make_async_remote_copy(
        src_ref=src, dst_ref=dst, send_sem=ss, recv_sem=rs, device_id=device, device_id_type=MESH
    ).start()


def wait(ref, sem):
    pltpu.make_async_copy(ref, ref, sem).wait()


class PlaneGather:
    def __init__(self, buf, ss, rs, me):
        self.buf, self.ss, self.rs, self.me = buf, ss, rs, me
        self.sent = []

    def shift(self, h, i, j):
        z, x, y, c = self.me
        dx, dy = (i, j) if h == 0 else (j, i)
        return wrap(x + dx), wrap(y + dy)

    def piece(self, h, spot, half=None):
        px, py = self.shift(h, *spot)
        row = h * 512 + (py * 4 + px) * 32
        if half is None:
            return self.buf.at[rows(row, 32)]
        return self.buf.at[rows(row + 16 * half, 16)]

    def spot(self, stage, i, j):
        return (j, 0) if stage == 0 else (i, j)

    def sem(self, h, stage, i, kind):
        return h * 20 + (0 if stage == 0 else 4 + 4 * (i % 4)) + kind

    def go(self, ref, h, stage, i, kind, step):
        s = self.sem(h, stage, i, kind)
        px, py = self.shift(h, *((step, 0) if stage == 0 else (0, step)))
        send(ref, ref, self.ss.at[s], self.rs.at[s], at(self.me[0], px, py, self.me[3]))
        self.sent.append((ref, s))

    def begin(self, h, stage, i=0):
        ref = self.piece(h, self.spot(stage, i, 0))
        self.go(ref, h, stage, i, 0, 1)
        self.go(ref, h, stage, i, 1, -1)

    def take(self, h, stage, i, kind):
        spot = self.spot(stage, i, (-1, 1)[kind])
        wait(self.piece(h, spot), self.rs.at[self.sem(h, stage, i, kind)])
        self.go(self.piece(h, spot, kind), h, stage, i, kind + 2, (1, -1)[kind])

    def relay(self, h, stage, i=0):
        self.take(h, stage, i, 0)
        self.take(h, stage, i, 1)

    def finish(self, h, stage, i=0):
        for kind in (2, 3):
            ref = self.piece(h, self.spot(stage, i, 2), kind - 2)
            wait(ref, self.rs.at[self.sem(h, stage, i, kind)])

    def first(self, h):
        self.begin(h, 0)
        self.begin(h, 1, 0)

    def steps(self):
        for h in (0, 1):
            self.take(h, 0, 0, 0)
            self.begin(h, 1, -1)
            self.take(h, 0, 0, 1)
            self.begin(h, 1, 1)
        yield
        for h in (0, 1):
            self.relay(h, 1, 0)
        for h in (0, 1):
            self.finish(h, 0)
            self.begin(h, 1, 2)
        yield
        for i in (-1, 1):
            for h in (0, 1):
                self.relay(h, 1, i)
            yield
        for h in (0, 1):
            self.relay(h, 1, 2)
        yield
        for i in (0, -1, 1, 2):
            for h in (0, 1):
                self.finish(h, 1, i)
        yield
        for ref, s in self.sent:
            wait(ref, self.ss.at[s])


class PlaneScatter(PlaneGather):
    def __init__(self, buf, halves, wholes, ss, rs, me):
        super().__init__(buf, ss, rs, me)
        self.halves, self.wholes = halves, wholes

    def ring(self, h, stage, i):
        return h * 5 + (0 if stage == 0 else 1 + i % 4)

    def post(self, ref, dst, h, stage, i, kind, step):
        s = self.sem(h, stage, i, kind)
        px, py = self.shift(h, *((step, 0) if stage == 0 else (0, step)))
        send(ref, dst, self.ss.at[s], self.rs.at[s], at(self.me[0], px, py, self.me[3]))
        self.sent.append((ref, s))

    def open(self, h, stage, i=0):
        r = self.ring(h, stage, i)
        for kind, step in ((0, 1), (1, -1)):
            ref = self.piece(h, self.spot(stage, i, 2), kind)
            self.post(ref, self.halves.at[r, kind], h, stage, i, kind, step)

    def middle(self, h, stage, i=0):
        r = self.ring(h, stage, i)
        for kind, step in ((0, 1), (1, -1)):
            got = self.halves.at[r, kind]
            wait(got, self.rs.at[self.sem(h, stage, i, kind)])
            own = self.piece(h, self.spot(stage, i, step), kind)
            own[...] = (own[...].astype(F32) + got[...].astype(F32)).astype(BF)
            ref = self.piece(h, self.spot(stage, i, step))
            self.post(ref, self.wholes.at[r, kind], h, stage, i, kind + 2, step)

    def close(self, h, stage, i=0):
        r = self.ring(h, stage, i)
        for kind in (0, 1):
            wait(self.wholes.at[r, kind], self.rs.at[self.sem(h, stage, i, kind + 2)])
        own = self.piece(h, self.spot(stage, i, 0))
        own[...] = (
            own[...].astype(F32)
            + self.wholes[r, 0].astype(F32)
            + self.wholes[r, 1].astype(F32)
        ).astype(BF)

    def begin_all(self):
        for i in (2, -1, 1, 0):
            for h in (0, 1):
                self.open(h, 1, i)

    def run(self):
        for i in (2, -1, 1, 0):
            for h in (0, 1):
                self.middle(h, 1, i)
        for h in (0, 1):
            self.close(h, 1, 2)
            self.open(h, 0)
        for i in (-1, 1):
            for h in (0, 1):
                self.close(h, 1, i)
        for h in (0, 1):
            self.middle(h, 0)
        for h in (0, 1):
            self.close(h, 1, 0)
        for h in (0, 1):
            self.close(h, 0)

    def done(self):
        for ref, s in self.sent:
            wait(ref, self.ss.at[s])


class Fourfold:
    def __init__(self, src, slot, ss, rs, me):
        self.src, self.slot, self.ss, self.rs, self.me = src, slot, ss, rs, me
        z, x, y, c = me
        self.core = lax.div(z, 2)
        self.own = self.core == c

    def start(self):
        z, x, y, c = self.me
        dst = self.slot(lax.rem(z, 2), c)
        r = lax.rem(z, 2) * 2 + c

        @pl.when(self.own)
        def _():
            pltpu.make_async_copy(self.src, dst, self.rs.at[r]).start()

        @pl.when(jnp.logical_not(self.own))
        def _():
            send(self.src, dst, self.ss.at[0], self.rs.at[r], at(z, x, y, self.core))

        for k in (1, 3, 2):
            send(self.src, dst, self.ss.at[k], self.rs.at[r], at(wrap(z + k), x, y, self.core))

    def arrive(self):
        for i in (0, 1):
            for j in (0, 1):
                wait(self.slot(i, j), self.rs.at[i * 2 + j])

    def done(self):
        @pl.when(jnp.logical_not(self.own))
        def _():
            wait(self.src, self.ss.at[0])

        for k in (1, 2, 3):
            wait(self.src, self.ss.at[k])


class Fold:
    def __init__(self, out, got, ss, rs, me):
        self.out, self.got, self.ss, self.rs, self.me = out, got, ss, rs, me

    def start(self, i, j):
        z, x, y, c = self.me
        p = i * 2 + j
        to = 2 * c + i
        own = jnp.logical_and(to == z, c == j)

        @pl.when(own)
        def _():
            pltpu.make_async_copy(self.out.at[p], self.got.at[z], self.rs.at[z]).start()

        @pl.when(jnp.logical_not(own))
        def _():
            send(self.out.at[p], self.got.at[z], self.ss.at[p], self.rs.at[z], at(to, x, y, j))

    def arrive(self):
        for i in range(4):
            wait(self.got.at[i], self.rs.at[i])

    def done(self):
        z, x, y, c = self.me
        for i in (0, 1):
            for j in (0, 1):
                own = jnp.logical_and(2 * c + i == z, c == j)

                @pl.when(jnp.logical_not(own))
                def _():
                    wait(self.out.at[i * 2 + j], self.ss.at[i * 2 + j])


class ChipSwap:
    def __init__(self, src, dst, ss, rs, me):
        self.src, self.dst, self.ss, self.rs, self.me = src, dst, ss, rs, me
        self.chip = me[2] * 4 + me[1]

    def start(self):
        z, x, y, c = self.me
        mine = self.chip

        def step(k, _):
            to = lax.rem(mine + k, 16)
            send(self.src(to), self.dst(mine), self.ss.at[k], self.rs.at[k], by_chip(z, to, c))
            return 0

        pltpu.make_async_copy(self.src(mine), self.dst(mine), self.rs.at[0]).start()
        lax.fori_loop(1, 16, step, 0)

    def arrive(self):
        def step(k, _):
            wait(self.dst(lax.rem(self.chip + 16 - k, 16)), self.rs.at[k])
            return 0

        lax.fori_loop(0, 16, step, 0)

    def done(self):
        def step(k, _):
            wait(self.src(lax.rem(self.chip + k, 16)), self.ss.at[k])
            return 0

        lax.fori_loop(1, 16, step, 0)


class DeviceSwap:
    def __init__(self, out, got, ss, rs, z):
        self.out, self.got, self.ss, self.rs, self.z = out, got, ss, rs, z
        self.e = lax.axis_index("expert")

    def start(self):
        mine = self.e

        def step(k, _):
            to = lax.rem(mine + k, 32)
            send(
                self.out.at[rows(16 * to, 16)],
                self.got.at[rows(16 * mine, 16)],
                self.ss.at[k],
                self.rs.at[k],
                {"group": self.z, "expert": to},
            )
            return 0

        pltpu.make_async_copy(
            self.out.at[rows(16 * mine, 16)], self.got.at[rows(16 * mine, 16)], self.rs.at[0]
        ).start()
        lax.fori_loop(1, 32, step, 0)

    def arrive(self):
        def step(k, _):
            wait(self.got.at[rows(16 * lax.rem(self.e + 32 - k, 32), 16)], self.rs.at[k])
            return 0

        lax.fori_loop(0, 32, step, 0)

    def done(self):
        def step(k, _):
            wait(self.out.at[rows(16 * lax.rem(self.e + k, 32), 16)], self.ss.at[k])
            return 0

        lax.fori_loop(1, 32, step, 0)


class DepthGather:
    def __init__(self, buf, cols, ss, rs, me):
        self.buf, self.cols, self.ss, self.rs, self.me = buf, cols, ss, rs, me

    def piece(self, step, half=None):
        row = 384 * wrap(self.me[0] + step)
        if half is None:
            return self.buf.at[rows(row, 384), self.cols]
        return self.buf.at[rows(row + 192 * half, 192), self.cols]

    def to(self, step):
        z, x, y, c = self.me
        return at(wrap(z + step), x, y, c)

    def start(self):
        own = self.piece(0)
        send(own, own, self.ss.at[0], self.rs.at[0], self.to(1))
        send(own, own, self.ss.at[1], self.rs.at[1], self.to(-1))

    def take(self, kind):
        step = (-1, 1)[kind]
        wait(self.piece(step), self.rs.at[kind])
        half = self.piece(step, kind)
        send(half, half, self.ss.at[2 + kind], self.rs.at[2 + kind], self.to(-step))

    def finish(self):
        for kind in (0, 1):
            wait(self.piece(2, kind), self.rs.at[2 + kind])

    def done(self):
        for kind in (0, 1):
            wait(self.piece(0), self.ss.at[kind])
            wait(self.piece((-1, 1)[kind], kind), self.ss.at[2 + kind])


class DepthScatter:
    def __init__(self, buf, cols, halves, wholes, ss, rs, me):
        self.buf, self.cols, self.halves, self.wholes = buf, cols, halves, wholes
        self.ss, self.rs, self.me = ss, rs, me

    def piece(self, step, half=None):
        row = 384 * wrap(self.me[0] + step)
        if half is None:
            return self.buf.at[rows(row, 384), self.cols]
        return self.buf.at[rows(row + 192 * half, 192), self.cols]

    def to(self, step):
        z, x, y, c = self.me
        return at(wrap(z + step), x, y, c)

    def open(self):
        for kind, step in ((0, 1), (1, -1)):
            send(self.piece(2, kind), self.halves.at[kind], self.ss.at[kind], self.rs.at[kind],
                 self.to(step))

    def middle(self):
        for kind, step in ((0, 1), (1, -1)):
            wait(self.halves.at[kind], self.rs.at[kind])
            own = self.piece(step, kind)
            own[...] = (own[...].astype(F32) + self.halves[kind].astype(F32)).astype(BF)
            send(self.piece(step), self.wholes.at[kind], self.ss.at[2 + kind],
                 self.rs.at[2 + kind], self.to(step))

    def close(self):
        for kind in (0, 1):
            wait(self.wholes.at[kind], self.rs.at[2 + kind])
        return (
            self.piece(0)[...].astype(F32)
            + self.wholes[0].astype(F32)
            + self.wholes[1].astype(F32)
        ).astype(BF)

    def done(self):
        for kind, step in ((0, 1), (1, -1)):
            wait(self.piece(2, kind), self.ss.at[kind])
            wait(self.piece(step), self.ss.at[2 + kind])


def dma(*shape):
    return pltpu.SemaphoreType.DMA(shape)


def iota(shape, dim):
    return lax.broadcasted_iota(jnp.int32, shape, dim)


def pick(condition):
    return jnp.where(condition, 1.0, 0.0)


def twelfth(value):
    return (value * 5462) >> 16


SCRATCH = dict(
    buf=((1024, 2048), BF), mwb=((256, 2048), BF), mc=((1024, 256), BF),
    sib_out=((512, 256), BF), sib_in=((512, 256), BF), tgc=((512, 256), BF), tgs=((128, 1024), BF),
    pg=((512, 128), BF), sel=((384, 512), BF),
    outb=((2, 512, 512), BF), inb=((2, 512, 512), BF),
    sc=((1536, 1024), BF), xv=((1536, 1024), BF), wi=((1024, 1024), BF), wo=((1024, 1024), BF),
    hid=((1536, 1024), BF), slope=((1536, 1024), F32), bg=((1536, 1024), BF), rp=((1536, 1024), BF),
    fb=((2, 2, 192, 512), BF), wb=((2, 2, 384, 512), BF),
    sgo=((4, 32, 128), BF), sgi=((4, 32, 128), BF),
    back=((2, 512, 512), BF), ret=((2, 512, 512), BF),
    hogs=((128, 1024), BF), hc=((1024, 256), BF), liv=((1024, 2048), BF), hwv=((2048, 256), BF),
    halves=((10, 2, 16, 2048), BF), wholes=((10, 2, 32, 2048), BF),
    hgo=((4, 1024, 128), BF), hgi=((4, 1024, 128), BF),
    mgo=((4, 128, 1024), BF), mgi=((4, 128, 1024), BF),
)
SEMS = dict(
    og_s=(40,), og_r=(40,), li_s=(40,), li_r=(40,), ig_s=(40,), ig_r=(40,),
    mw_s=(4,), mw_r=(4,), hw_s=(4,), hw_r=(4,),
    mc_s=(16,), mc_r=(16,), tk_s=(16,), tk_r=(16,), hc_s=(16,), hc_r=(16,),
    to_s=(2, 32), to_r=(2, 32), fr_s=(2, 32), fr_r=(2, 32),
    xv_s=(4,), xv_r=(4,), sc_s=(2, 4), sc_r=(2, 4), rp_s=(2, 4), rp_r=(2, 4),
    sg_s=(4,), sg_r=(4,), mg_s=(4,), mg_r=(4,), hg_s=(4,), hg_r=(4,),
    local=(8,), sib_s=(8,), sib_r=(8,),
)
NAMES = list(SCRATCH) + list(SEMS)


class Named:
    def __init__(self, names, refs):
        for name, ref in zip(names, refs, strict=True):
            setattr(self, name, ref)


def kernel(og, mw, merged, disp, w_in, w_out, li, hw, ids, gates,
           ig, hg, mg, ing, outg, gg, *refs):
    v = Named(NAMES, refs)
    me = place()
    z, x, y, c = me
    chip = y * 4 + x
    e = chip * 2 + c
    other = at(z, x, y, 1 - c)

    barrier = pltpu.get_barrier_semaphore()

    def greet(k, _):
        pl.semaphore_signal(
            barrier, inc=1, device_id={"group": z, "expert": lax.rem(e + k, 32)},
            device_id_type=MESH,
        )
        return 0

    lax.fori_loop(1, 32, greet, 0)
    for step in (1, 2, 3):
        for core in (0, 1):
            pl.semaphore_signal(
                barrier, inc=1, device_id=at(wrap(z + step), x, y, core), device_id_type=MESH
            )

    def local(src, dst, k):
        copy = pltpu.make_async_copy(src, dst, v.local.at[k])
        copy.start()
        return copy

    mine = rows(c * 512 + chip * 32, 32)
    theirs = rows((1 - c) * 512 + chip * 32, 32)
    own_half, other_half = lanes(c * 2048, 2048), lanes((1 - c) * 2048, 2048)
    own_rows = rows(384 * z, 384)
    og_load = local(og.at[:, own_half], v.buf.at[mine], 0)
    xv_load = local(disp, v.xv.at[own_rows], 1)
    li_load = local(li.at[:, own_half], v.liv.at[mine], 2)
    wi_load = local(w_in, v.wi, 3)
    wo_load = local(w_out, v.wo, 4)

    names = [pick(iota((32, 128), 0) == ids[k:k + 1, :]) for k in (0, 1)]
    before = pick(iota((128, 128), 0) < iota((128, 128), 1)).astype(BF)
    counts = dot((names[0] + names[1]).astype(BF), before, NN)
    ranks = [jnp.sum(name * counts, axis=0, keepdims=True) for name in names]
    slots = iota((512, 128), 0).astype(F32)
    table = jnp.zeros((512, 128), F32)
    for k in (0, 1):
        target = ids[k:k + 1, :].astype(F32) * 16.0 + ranks[k]
        table = table + jnp.where(slots == target, gates[k:k + 1, :], 0.0)
    source = iota((128, 128), 0)
    order = pick(iota((128, 128), 1) == (source & 3) * 32 + (source >> 2)).astype(BF)
    v.pg[...] = dot(table.astype(BF), order, NN).astype(BF)
    row = iota((384, 512), 0)
    v.sel[...] = pick(iota((384, 512), 1) == row + 4 * twelfth(row)).astype(BF)

    pl.semaphore_wait(barrier, 37)

    send(og.at[:, other_half], v.buf.at[mine], v.sib_s.at[0], v.sib_r.at[0], other)
    weights = Fourfold(
        mw, lambda i, j: v.mwb.at[rows(128 * j, 128), lanes(1024 * i, 1024)], v.mw_s, v.mw_r, me
    )
    weights.start()
    og_load.wait()
    wait(v.buf.at[theirs], v.sib_r.at[0])
    gather = PlaneGather(v.buf, v.og_s, v.og_r, me)
    for h in (0, 1):
        gather.first(h)
    columns = ChipSwap(
        lambda to: merged.at[:, lanes(256 * to, 256)],
        lambda k: v.mc.at[rows(c * 512 + k * 32, 32)],
        v.mc_s, v.mc_r, me,
    )
    columns.start()
    xv_load.wait()
    inputs = DepthGather(v.xv, pl.ds(0, 1024), v.xv_s, v.xv_r, me)
    inputs.start()
    send(li.at[:, other_half], v.liv.at[mine], v.sib_s.at[1], v.sib_r.at[1], other)
    for _ in gather.steps():
        pass
    weights.arrive()

    def product(h, tile):
        return dot(v.buf[rows(h * 512 + tile * 256, 256), :], v.mwb[...], NT)

    for tile in (0, 1):
        v.sib_out[pl.ds(tile * 256, 256), :] = product(1 - c, tile).astype(BF)
    send(v.sib_out, v.sib_in, v.sib_s.at[2], v.sib_r.at[2], other)
    own = [product(c, tile) for tile in (0, 1)]
    wait(v.sib_in, v.sib_r.at[2])
    for tile in (0, 1):
        part = pl.ds(tile * 256, 256)
        v.tgc[part, :] = (own[tile] + v.sib_in[part, :].astype(F32)).astype(BF)
    tokens = ChipSwap(
        lambda to: v.tgc.at[rows(32 * to, 32)],
        lambda k: v.tgs.at[rows(32 * lax.div(k, 4), 32), lanes(256 * lax.rem(k, 4), 256)],
        v.tk_s, v.tk_r, me,
    )
    tokens.start()
    inputs.take(0)
    inputs.take(1)
    columns.arrive()
    mc_half = v.mc.at[rows(c * 512, 512)]
    send(mc_half, mc_half, v.sib_s.at[3], v.sib_r.at[3], other)
    wi_load.wait()

    def early(step):
        def tile(t, _):
            part = rows(384 * wrap(z + step) + 192 * t, 192)
            value, grade = gelu_pair(dot(v.xv[part, :], v.wi[...], NN))
            v.hid[part, :] = value.astype(BF)
            v.slope[part, :] = grade
            return 0

        lax.fori_loop(0, 2, tile, 0)

    early(0)
    tokens.arrive()

    there, spread = [], []
    for p in (0, 1):
        v.outb[p] = dot(v.pg[...], v.tgs[:, 512 * p:512 * p + 512], NN).astype(BF)
        there.append(DeviceSwap(v.outb.at[p], v.inb.at[p], v.to_s.at[p], v.to_r.at[p], z))
        there[p].start()
        spread.append(
            DepthGather(v.sc, pl.ds(512 * p, 512), v.sc_s.at[p], v.sc_r.at[p], me)
        )
    early(1)
    early(3)
    wait(v.mc.at[rows((1 - c) * 512, 512)], v.sib_r.at[3])
    for p in (0, 1):
        there[p].arrive()
        v.sc[own_rows, 512 * p:512 * p + 512] = dot(v.sel[...], v.inb[p], NN).astype(BF)
        spread[p].start()
    li_load.wait()
    wait(v.liv.at[theirs], v.sib_r.at[1])
    gather_li = PlaneGather(v.liv, v.li_s, v.li_r, me)
    for h in (0, 1):
        gather_li.first(h)
    progress = gather_li.steps()
    inputs.finish()
    early(2)
    wo_load.wait()
    block = twelfth(iota((32, 384), 1))
    sums = pick(iota((32, 384), 0) == block).astype(BF)
    tall = iota((384, 128), 0)
    mask = pick(iota((384, 128), 1) == tall - 12 * twelfth(tall))

    def chunk(step):
        q = wrap(z + step)
        part = rows(384 * q, 384)
        grad = dot(v.sc[part, :], v.wo[...], NT)
        column = jnp.sum(grad * v.hid[part, :].astype(F32), axis=1, keepdims=True)
        v.sgo[q] = dot(sums, (column * mask).astype(BF), NN).astype(BF)
        v.bg[part, :] = (grad * v.slope[part, :]).astype(BF)
        if step:
            send(v.sgo.at[q], v.sgi.at[z], v.sg_s.at[step], v.sg_r.at[4 - step], at(q, x, y, c))

    def back_rows(step, p):
        part = rows(384 * wrap(z + step), 384)
        v.rp[part, 512 * p:512 * p + 512] = dot(
            v.bg[part, :], v.wi[512 * p:512 * p + 512, :], NT
        ).astype(BF)

    chunk(0)
    next(progress)
    for p in (0, 1):
        spread[p].take(0)
        spread[p].take(1)
    for p in (0, 1):
        back_rows(0, p)
    next(progress)
    for step in (1, 3):
        chunk(step)
        for p in (0, 1):
            back_rows(step, p)
    next(progress)
    for p in (0, 1):
        spread[p].finish()
    chunk(2)
    gathered = [
        DepthScatter(v.rp, pl.ds(512 * p, 512), v.fb.at[p], v.wb.at[p], v.rp_s.at[p], v.rp_r.at[p],
                     me)
        for p in (0, 1)
    ]
    for p in (0, 1):
        back_rows(2, p)
        gathered[p].open()
    next(progress)
    for p in (0, 1):
        gathered[p].middle()
    next(progress)

    def weight(t, _):
        part = lanes(256 * t, 256)
        ing[:, part] = dot(v.xv[...], v.bg[:, part], TN).astype(BF)
        outg[:, part] = dot(v.hid[...], v.sc[:, part], TN).astype(BF)
        return 0

    lax.fori_loop(0, 4, weight, 0)
    for tile in range(4):
        total = dot(v.mc[...], v.buf[:, tile * 512:tile * 512 + 512], TN).astype(BF)
        for j in (0, 1):
            v.mgo[(tile // 2) * 2 + j, :, (tile % 2) * 512:(tile % 2) * 512 + 512] = total[
                128 * j:128 * j + 128
            ]
    for step in (1, 2, 3):
        wait(v.sgi.at[wrap(z + step)], v.sg_r.at[step])
    marks = v.sgo[z].astype(F32)
    for step in (1, 2, 3):
        marks = marks + v.sgi[wrap(z + step)].astype(F32)
    last = pick(iota((512, 32), 0) == iota((512, 32), 1) * 16 + 12).astype(BF)
    marks = dot(last, marks.astype(BF), NN)
    home = []
    for p in (0, 1):
        v.back[p] = dot(v.sel[...], gathered[p].close(), TN).astype(BF)
        if p == 0:
            v.back[0, :, 0:128] = (v.back[0, :, 0:128].astype(F32) + marks).astype(BF)
        home.append(DeviceSwap(v.back.at[p], v.ret.at[p], v.fr_s.at[p], v.fr_r.at[p], z))
        home[p].start()
    head_weights = Fourfold(
        hw, lambda i, j: v.hwv.at[rows(1024 * i, 1024), lanes(128 * j, 128)], v.hw_s, v.hw_r, me
    )
    head_weights.start()
    merge_sum = Fold(v.mgo, v.mgi, v.mg_s, v.mg_r, me)
    for i in (0, 1):
        for j in (0, 1):
            merge_sum.start(i, j)
    for _ in progress:
        pass

    for p in (0, 1):
        home[p].arrive()
        v.hogs[:, 512 * p:512 * p + 512] = dot(v.pg[...], v.ret[p], TN).astype(BF)
    hog_columns = ChipSwap(
        lambda to: v.hogs.at[rows(32 * lax.div(to, 4), 32), lanes(256 * lax.rem(to, 4), 256)],
        lambda k: v.hc.at[rows(c * 512 + k * 32, 32)],
        v.hc_s, v.hc_r, me,
    )
    hog_columns.start()
    found = dot(last, v.ret[0, :, 0:128], TN).astype(BF)
    for k in (0, 1):
        value = dot(found, names[k].astype(BF), TN)
        value = jnp.where(iota((128, 128), 0).astype(F32) == ranks[k], value, 0.0)
        gg[k:k + 1, :] = jnp.sum(value, axis=0, keepdims=True) / gates[k:k + 1, :]
    head_weights.arrive()
    hog_columns.arrive()
    hc_half = v.hc.at[rows(c * 512, 512)]
    send(hc_half, hc_half, v.sib_s.at[4], v.sib_r.at[4], other)

    def product_out(h):
        def step(t, _):
            tile = rows(h * 512 + 128 * t, 128)
            v.buf[tile, :] = dot(v.hc[tile, :], v.hwv[...], NT).astype(BF)
            return 0

        lax.fori_loop(0, 4, step, 0)

    product_out(c)
    wait(v.hc.at[rows((1 - c) * 512, 512)], v.sib_r.at[4])
    product_out(1 - c)
    scatter = PlaneScatter(v.buf, v.halves, v.wholes, v.ig_s, v.ig_r, me)
    scatter.begin_all()
    head_sum = Fold(v.hgo, v.hgi, v.hg_s, v.hg_r, me)
    for i in (0, 1):
        for tile in (0, 1):
            first = i * 1024 + tile * 512
            total = dot(v.liv[:, first:first + 512], v.hc[...], TN)
            for j in (0, 1):
                v.hgo[i * 2 + j, tile * 512:tile * 512 + 512, :] = total[
                    :, 128 * j:128 * j + 128
                ].astype(BF)
        for j in (0, 1):
            head_sum.start(i, j)
    scatter.run()
    give, keep = v.buf.at[theirs], v.buf.at[mine]
    send(give, ig.at[:, own_half], v.sib_s.at[5], v.sib_r.at[5], other)
    ig_keep = local(keep, ig.at[:, own_half], 5)
    merge_sum.arrive()
    mg[...] = (v.mgi[0].astype(F32) + v.mgi[1].astype(F32)) + (
        v.mgi[2].astype(F32) + v.mgi[3].astype(F32)
    )
    head_sum.arrive()
    hg[...] = (v.hgi[0].astype(F32) + v.hgi[1].astype(F32)) + (
        v.hgi[2].astype(F32) + v.hgi[3].astype(F32)
    )
    wait(ig.at[:, other_half], v.sib_r.at[5])
    ig_keep.wait()
    for part in (weights, columns, inputs, tokens, *there, *spread, *gathered, *home,
                 head_weights, merge_sum, hog_columns, head_sum, scatter):
        part.done()
    for step in (1, 2, 3):
        wait(v.sgo.at[wrap(z + step)], v.sg_s.at[step])
    for k, ref in enumerate((v.buf.at[mine], v.liv.at[mine], v.sib_out, mc_half, hc_half, give)):
        wait(ref, v.sib_s.at[k])


VM = pl.BlockSpec(memory_space=pltpu.VMEM)
ANY = pl.BlockSpec(memory_space=pl.ANY)


def body(
    layer_input, out_grad, merged, head_weight, merge_weight,
    expert_in, expert_out, dispatched, expert_ids, gate_values,
):
    outs = (
        ((32, 4096), BF), ((1024, 128), F32), ((128, 1024), F32),
        ((1024, 1024), BF), ((1024, 1024), BF), ((2, 128), F32),
    )
    input_total, head_grad, merge_grad, in_grad, out_weight_grad, gate_grad = pl.pallas_call(
        kernel,
        out_shape=[jax.ShapeDtypeStruct(shape, kind) for shape, kind in outs],
        in_specs=[ANY] * 8 + [VM] * 2,
        out_specs=[VM] * 6,
        scratch_shapes=[pltpu.VMEM(*kind) for kind in SCRATCH.values()]
        + [dma(*shape) for shape in SEMS.values()],
        compiler_params=pltpu.CompilerParams(
            has_side_effects=True, collective_id=0, vmem_limit_bytes=LIMIT
        ),
        cost_estimate=pl.CostEstimate(flops=1 << 35, bytes_accessed=1 << 25, transcendentals=0),
    )(
        out_grad, merge_weight, merged, dispatched[0], expert_in[0], expert_out[0],
        layer_input, head_weight, expert_ids.T, gate_values.T.astype(F32),
    )
    return (
        input_total,
        head_grad,
        merge_grad,
        in_grad[None].astype(F32),
        out_weight_grad[None].astype(F32),
        gate_grad.T.astype(BF),
    )


def solution(mesh):
    placed = (
        P(("group", "expert"), None),
        P(("group", "expert"), None),
        P(("group", "expert"), None),
        P("group", "expert"),
        P("expert", "group"),
        P("expert", None, "group"),
        P("expert", "group", None),
        P("expert", "group", None),
        P(("group", "expert"), None),
        P(("group", "expert"), None),
    )
    return jax.shard_map(
        body,
        mesh=mesh,
        in_specs=placed,
        out_specs=(
            P(("group", "expert"), None),
            P("group", "expert"),
            P("expert", "group"),
            P("expert", None, "group"),
            P("expert", "group", None),
            P(("group", "expert"), None),
        ),
        check_vma=False,
    )
```

```python
import jax
import jax.numpy as jnp
from jax import lax
from jax.experimental import pallas as pl
from jax.experimental.pallas import tpu as pltpu
from jax.sharding import PartitionSpec as P

MESH = pl.DeviceIdType.MESH
BF = jnp.bfloat16
F32 = jnp.float32
LIMIT = 63 << 20

root_scale = 0.7978845608028654
cubic_term = 0.044715


def gelu_pair(value):
    square = value * value
    tangent = jnp.tanh(root_scale * value * (1.0 + cubic_term * square))
    half = 0.5 * (1.0 + tangent)
    slope = half + 0.5 * value * (1.0 - tangent * tangent) * root_scale * (
        1.0 + 3.0 * cubic_term * square
    )
    return value * half, slope


def dot(left, right, dims):
    return lax.dot_general(left, right, ((dims[:1], dims[1:]), ((), ())), preferred_element_type=F32)


NN, NT, TN = (1, 0), (1, 1), (0, 0)


def wrap(value):
    return lax.rem(value + 8, 4)


def place():
    e = lax.axis_index("expert")
    return lax.axis_index("group"), lax.rem(lax.div(e, 2), 4), lax.div(e, 8), lax.rem(e, 2)


def at(z, x, y, c):
    return {"group": z, "expert": (y * 4 + x) * 2 + c}


def by_chip(z, chip, c):
    return {"group": z, "expert": chip * 2 + c}


def rows(start, size):
    return pl.ds(pl.multiple_of(start, 16), size)


def lanes(start, size):
    return pl.ds(pl.multiple_of(start, 128), size)


def send(src, dst, ss, rs, device):
    pltpu.make_async_remote_copy(
        src_ref=src, dst_ref=dst, send_sem=ss, recv_sem=rs, device_id=device, device_id_type=MESH
    ).start()


def wait(ref, sem):
    pltpu.make_async_copy(ref, ref, sem).wait()


class PlaneGather:
    def __init__(self, buf, base, ss, rs, me):
        self.buf, self.base, self.ss, self.rs, self.me = buf, base, ss, rs, me

    def shift(self, h, i, j):
        z, x, y, c = self.me
        dx, dy = (i, j) if h == 0 else (j, i)
        return wrap(x + dx), wrap(y + dy)

    def piece(self, h, spot, half=None):
        px, py = self.shift(h, *spot)
        row = self.base + (py * 4 + px) * 32 + h * 16
        if half is None:
            return self.buf.at[rows(row, 16)]
        return self.buf.at[rows(row, 16), half * 1024:half * 1024 + 1024]

    def spot(self, stage, i, j):
        return (j, 0) if stage == 0 else (i, j)

    def ring(self, h, stage, i):
        return h * 5 + (0 if stage == 0 else 1 + i % 4)

    def sem(self, h, stage, i, kind):
        return self.rs.at[self.ring(h, stage, i) * 3 + min(kind, 2)]

    def post(self, ref, dst, h, stage, i, kind, step):
        px, py = self.shift(h, *((step, 0) if stage == 0 else (0, step)))
        send(ref, dst, self.ss, self.sem(h, stage, i, kind), at(self.me[0], px, py, self.me[3]))

    def begin(self, h, stage, i=0):
        ref = self.piece(h, self.spot(stage, i, 0))
        self.post(ref, ref, h, stage, i, 0, 1)
        self.post(ref, ref, h, stage, i, 1, -1)

    def take(self, h, stage, i, kind):
        spot = self.spot(stage, i, (-1, 1)[kind])
        wait(self.piece(h, spot), self.sem(h, stage, i, kind))
        ref = self.piece(h, spot, kind)
        self.post(ref, ref, h, stage, i, kind + 2, (1, -1)[kind])

    def relay(self, h, stage, i=0):
        self.take(h, stage, i, 0)
        self.take(h, stage, i, 1)

    def close(self, h, stage, i=0):
        wait(self.piece(h, self.spot(stage, i, 2)), self.sem(h, stage, i, 2))

    def first(self):
        for h in (0, 1):
            self.begin(h, 0)
            self.begin(h, 1, 0)

    def steps(self):
        for h in (0, 1):
            self.take(h, 0, 0, 0)
            self.begin(h, 1, -1)
            self.take(h, 0, 0, 1)
            self.begin(h, 1, 1)
        yield
        for h in (0, 1):
            self.relay(h, 1, 0)
        for h in (0, 1):
            self.close(h, 0)
            self.begin(h, 1, 2)
        yield
        for i in (-1, 1):
            for h in (0, 1):
                self.relay(h, 1, i)
            yield
        for h in (0, 1):
            self.relay(h, 1, 2)
        yield

    def finish(self):
        for i in (0, -1, 1, 2):
            for h in (0, 1):
                self.close(h, 1, i)

    def done(self):
        wait(self.buf.at[self.base:self.base + 480], self.ss)


class PlaneScatter(PlaneGather):
    def __init__(self, buf, base, halves, wholes, ss, rs, me):
        super().__init__(buf, base, ss, rs, me)
        self.halves, self.wholes = halves, wholes

    def sem(self, h, stage, i, kind):
        return self.rs.at[self.ring(h, stage, i) * 2 + kind // 2]

    def open(self, h, stage, i=0):
        r = self.ring(h, stage, i)
        for kind, step in ((0, 1), (1, -1)):
            ref = self.piece(h, self.spot(stage, i, 2), kind)
            self.post(ref, self.halves.at[r, kind], h, stage, i, kind, step)

    def middle(self, h, stage, i=0):
        r = self.ring(h, stage, i)
        wait(self.halves.at[r], self.sem(h, stage, i, 0))
        for kind, step in ((0, 1), (1, -1)):
            got = self.halves.at[r, kind]
            own = self.piece(h, self.spot(stage, i, step), kind)
            own[...] = (own[...].astype(F32) + got[...].astype(F32)).astype(BF)
            ref = self.piece(h, self.spot(stage, i, step))
            self.post(ref, self.wholes.at[r, kind], h, stage, i, kind + 2, step)

    def add(self, h, stage, i=0):
        r = self.ring(h, stage, i)
        wait(self.wholes.at[r], self.sem(h, stage, i, 2))
        own = self.piece(h, self.spot(stage, i, 0))
        own[...] = (
            own[...].astype(F32)
            + self.wholes[r, 0].astype(F32)
            + self.wholes[r, 1].astype(F32)
        ).astype(BF)

    def first(self):
        for i in (2, -1, 1, 0):
            for h in (0, 1):
                self.open(h, 1, i)

    def steps(self):
        for i in (2, -1, 1, 0):
            for h in (0, 1):
                self.middle(h, 1, i)
        yield
        for h in (0, 1):
            self.add(h, 1, 2)
            self.open(h, 0)
        for i in (-1, 1):
            for h in (0, 1):
                self.add(h, 1, i)
        yield
        for h in (0, 1):
            self.middle(h, 0)
        for h in (0, 1):
            self.add(h, 1, 0)
        yield
        for h in (0, 1):
            self.add(h, 0)
        yield


class Fourfold:
    def __init__(self, src, slot, dst, ss, rs, me):
        self.src, self.slot, self.dst, self.ss, self.rs, self.me = src, slot, dst, ss, rs, me
        z, x, y, c = me
        self.core = lax.div(z, 2)
        self.own = self.core == c

    def start(self):
        z, x, y, c = self.me
        dst = self.slot(lax.rem(z, 2), c)
        @pl.when(self.own)
        def _():
            pltpu.make_async_copy(self.src, dst, self.rs).start()

        @pl.when(jnp.logical_not(self.own))
        def _():
            send(self.src, dst, self.ss.at[1], self.rs, at(z, x, y, self.core))

        for k in (1, 3, 2):
            send(self.src, dst, self.ss.at[0], self.rs, at(wrap(z + k), x, y, self.core))

    def arrive(self):
        wait(self.dst, self.rs)

    def done(self):
        @pl.when(jnp.logical_not(self.own))
        def _():
            wait(self.src, self.ss.at[1])

        wait(self.dst.at[0:self.dst.shape[0] * 3 // 4], self.ss.at[0])


class Fold:
    def __init__(self, out, got, ss, rs, me):
        self.out, self.got, self.ss, self.rs, self.me = out, got, ss, rs, me

    def start(self, i, j):
        z, x, y, c = self.me
        p = i * 2 + j
        to = 2 * c + i
        own = jnp.logical_and(to == z, c == j)

        @pl.when(own)
        def _():
            pltpu.make_async_copy(self.out.at[p], self.got.at[z], self.rs).start()

        @pl.when(jnp.logical_not(own))
        def _():
            send(self.out.at[p], self.got.at[z], self.ss, self.rs, at(to, x, y, j))

    def arrive(self):
        wait(self.got, self.rs)

    def done(self):
        z, x, y, c = self.me
        own = lax.div(z, 2) == c

        @pl.when(own)
        def _():
            wait(self.out.at[0:3], self.ss)

        @pl.when(jnp.logical_not(own))
        def _():
            wait(self.out, self.ss)


class ChipSwap:
    def __init__(self, src, dst, size, ss, rs, me):
        self.src, self.dst, self.size, self.ss, self.rs, self.me = src, dst, size, ss, rs, me
        self.chip = me[2] * 4 + me[1]

    def start(self):
        z, x, y, c = self.me
        mine = self.chip

        def step(k, _):
            to = lax.rem(mine + k, 16)
            send(self.src(to), self.dst(mine), self.ss, self.rs, by_chip(z, to, c))
            return 0

        pltpu.make_async_copy(self.src(mine), self.dst(mine), self.rs).start()
        lax.fori_loop(1, 16, step, 0)

    def arrive(self):
        wait(self.size.at[0:512], self.rs)

    def done(self):
        wait(self.size.at[0:480], self.ss)


class Dispatch:
    def __init__(self, out, got, ss, rs, me):
        self.out, self.got, self.ss, self.rs, self.me = out, got, ss, rs, me
        self.chip = me[2] * 4 + me[1]
        self.e = self.chip * 2 + me[3]

    def start(self):
        dst, sem = self.got.at[rows(16 * self.chip, 16)], self.rs

        def step(k, _):
            to = lax.rem(self.e + k, 32)
            send(self.out.at[rows(16 * to, 16)], dst, self.ss, sem,
                 {"group": self.me[0], "expert": to})
            return 0

        pltpu.make_async_copy(self.out.at[rows(16 * self.e, 16)], dst, sem).start()
        lax.fori_loop(1, 32, step, 0)

    def arrive(self):
        wait(self.got, self.rs)


class Return:
    def __init__(self, out, got, half, ss, rs, me):
        self.out, self.got, self.half, self.ss, self.rs, self.me = out, got, half, ss, rs, me
        self.chip = me[2] * 4 + me[1]
        self.e = self.chip * 2 + me[3]

    def start(self):
        dst, sem = self.got.at[rows(16 * self.e, 16)], self.rs

        def step(k, _):
            to = lax.rem(self.chip + k, 16)
            send(self.out.at[rows(16 * to, 16)], dst, self.ss.at[0], sem,
                 by_chip(self.me[0], to, self.half))
            return 0

        lax.fori_loop(1, 16, step, 0)
        own = self.out.at[rows(16 * self.chip, 16)]

        @pl.when(self.me[3] == self.half)
        def _():
            pltpu.make_async_copy(own, dst, sem).start()

        @pl.when(self.me[3] != self.half)
        def _():
            send(own, dst, self.ss.at[1], sem, by_chip(self.me[0], self.chip, self.half))

    def arrive(self):
        wait(self.got, self.rs)

    def done(self):
        wait(self.out.at[0:240], self.ss.at[0])

        @pl.when(self.me[3] != self.half)
        def _():
            wait(self.out.at[0:16], self.ss.at[1])


class DepthGather:
    def __init__(self, buf, base, size, ss, rs, me):
        self.buf, self.base, self.size, self.ss, self.rs, self.me = buf, base, size, ss, rs, me

    def piece(self, step, half=None):
        row = 384 * wrap(self.me[0] + step) + self.base
        if half is None:
            return self.buf.at[rows(row, self.size)]
        return self.buf.at[rows(row + self.size // 2 * half, self.size // 2)]

    def to(self, step):
        z, x, y, c = self.me
        return at(wrap(z + step), x, y, c)

    def start(self):
        own = self.piece(0)
        send(own, own, self.ss, self.rs.at[0], self.to(1))
        send(own, own, self.ss, self.rs.at[1], self.to(-1))

    def take(self):
        for kind, step in ((0, -1), (1, 1)):
            wait(self.piece(step), self.rs.at[kind])
            half = self.piece(step, kind)
            send(half, half, self.ss, self.rs.at[2], self.to(-step))

    def finish(self):
        wait(self.piece(2), self.rs.at[2])

    def done(self):
        wait(self.buf.at[0:3 * self.size], self.ss)


class DepthScatter(DepthGather):
    def __init__(self, buf, base, size, halves, wholes, ss, rs, me):
        super().__init__(buf, base, size, ss, rs, me)
        self.halves, self.wholes = halves, wholes

    def open(self):
        for kind, step in ((0, 1), (1, -1)):
            send(self.piece(2, kind), self.halves.at[kind], self.ss, self.rs.at[0], self.to(step))

    def middle(self):
        wait(self.halves, self.rs.at[0])
        for kind, step in ((0, 1), (1, -1)):
            own = self.piece(step, kind)
            own[...] = (own[...].astype(F32) + self.halves[kind].astype(F32)).astype(BF)
            send(self.piece(step), self.wholes.at[kind], self.ss, self.rs.at[1], self.to(step))

    def total(self):
        wait(self.wholes, self.rs.at[1])
        return (
            self.piece(0)[...].astype(F32)
            + self.wholes[0].astype(F32)
            + self.wholes[1].astype(F32)
        ).astype(BF)


def dma(*shape):
    return pltpu.SemaphoreType.DMA(shape)


def iota(shape, dim):
    return lax.broadcasted_iota(jnp.int32, shape, dim)


def pick(condition):
    return jnp.where(condition, 1.0, 0.0)


def twelfth(value):
    return (value * 5462) >> 16


SCRATCH = dict(
    buf=((1024, 2048), BF), mwb=((256, 2048), BF), mc=((1024, 256), BF),
    sib_out=((512, 256), BF), sib_in=((512, 256), BF), tgc=((512, 256), BF), tgs=((128, 1024), BF),
    pg=((512, 128), BF), sel=((192, 256), BF),
    outb=((512, 1024), BF), inb=((2, 256, 1024), BF),
    sc=((1536, 1024), BF), xv=((1536, 1024), BF), wi=((1024, 1024), BF), wo=((1024, 1024), BF),
    hid=((1536, 1024), BF), slope=((1536, 1024), F32), bg=((1536, 1024), BF), rp=((1536, 1024), BF),
    fb=((2, 2, 96, 1024), BF), wb=((2, 2, 192, 1024), BF),
    sgo=((2, 4, 16, 128), BF), sgi=((2, 4, 16, 128), BF),
    back=((2, 256, 1024), BF), ret=((512, 1024), BF),
    hogs=((128, 1024), BF), hc=((1024, 256), BF), liv=((1024, 2048), BF), hwv=((2048, 256), BF),
    halves=((2, 10, 2, 16, 1024), BF), wholes=((2, 10, 2, 16, 2048), BF),
    hgo=((4, 1024, 128), BF), hgi=((4, 1024, 128), BF),
    mgo=((4, 128, 1024), BF), mgi=((4, 128, 1024), BF),
    ingv=((1024, 1024), BF), outgv=((1024, 1024), BF),
)
SEMS = dict(
    og_s=(2,), og_r=(2, 30), li_s=(2,), li_r=(2, 30), ig_s=(2,), ig_r=(2, 20),
    mw_s=(2,), mw_r=(1,), hw_s=(2,), hw_r=(1,),
    mc_s=(1,), mc_r=(1,), tk_s=(1,), tk_r=(1,), hc_s=(1,), hc_r=(1,),
    to_s=(1,), to_r=(2,), fr_s=(2, 2), fr_r=(1,),
    xv_s=(1,), xv_r=(3,), sc_s=(2,), sc_r=(2, 3), rp_s=(2,), rp_r=(2, 2),
    sg_s=(2,), sg_r=(2,), mg_s=(1,), mg_r=(1,), hg_s=(1,), hg_r=(1,),
    local=(6,), out=(2,), sib_s=(6,), sib_r=(6,),
)
NAMES = list(SCRATCH) + list(SEMS)


class Named:
    def __init__(self, names, refs):
        for name, ref in zip(names, refs, strict=True):
            setattr(self, name, ref)


def kernel(og, mw, merged, disp, w_in, w_out, li, hw, ids, gates,
           ig, hg, mg, ing, outg, gg, *refs):
    v = Named(NAMES, refs)
    me = place()
    z, x, y, c = me
    chip = y * 4 + x
    e = chip * 2 + c
    other = at(z, x, y, 1 - c)

    barrier = pltpu.get_barrier_semaphore()

    def greet(k, _):
        pl.semaphore_signal(
            barrier, inc=1, device_id={"group": z, "expert": lax.rem(e + k, 32)},
            device_id_type=MESH,
        )
        return 0

    lax.fori_loop(1, 32, greet, 0)
    for step in (1, 2, 3):
        for core in (0, 1):
            pl.semaphore_signal(
                barrier, inc=1, device_id=at(wrap(z + step), x, y, core), device_id_type=MESH
            )

    def local(src, dst, k):
        copy = pltpu.make_async_copy(src, dst, v.local.at[k])
        copy.start()
        return copy

    mine = rows(c * 512 + chip * 32, 32)
    theirs = rows((1 - c) * 512 + chip * 32, 32)
    own_half, other_half = lanes(c * 2048, 2048), lanes((1 - c) * 2048, 2048)
    own_rows = rows(384 * z, 384)
    raw = v.rp.at[0:384]
    xv_load = local(disp, raw, 1)
    og_load = local(og.at[:, own_half], v.buf.at[mine], 0)
    wi_load = local(w_in, v.wi, 3)
    li_load = local(li.at[:, own_half], v.liv.at[mine], 2)
    wo_load = local(w_out, v.wo, 4)

    row = iota((384, 384), 0)
    late = (row >= 192).astype(jnp.int32)
    first = row - 192 * late
    order = pick(iota((384, 384), 1) == first + 12 * twelfth(first) + 12 * late).astype(BF)
    xv_load.wait()
    v.xv[own_rows, :] = dot(order, raw[...], NN).astype(BF)
    pl.semaphore_wait(barrier, 37)

    send(og.at[:, other_half], v.buf.at[mine], v.sib_s.at[0], v.sib_r.at[0], other)
    weights = Fourfold(
        mw, lambda i, j: v.mwb.at[rows(128 * j, 128), lanes(1024 * i, 1024)], v.mwb,
        v.mw_s, v.mw_r.at[0], me,
    )
    weights.start()
    gather = [PlaneGather(v.buf, 512 * h, v.og_s.at[h], v.og_r.at[h], me) for h in (0, 1)]
    gather_li = [PlaneGather(v.liv, 512 * h, v.li_s.at[h], v.li_r.at[h], me) for h in (0, 1)]
    og_load.wait()
    wait(v.buf.at[theirs], v.sib_r.at[0])
    gather[0].first()

    names = [pick(iota((32, 128), 0) == ids[k:k + 1, :]) for k in (0, 1)]
    before = pick(iota((128, 128), 0) < iota((128, 128), 1)).astype(BF)
    counts = dot((names[0] + names[1]).astype(BF), before, NN)
    ranks = [jnp.sum(name * counts, axis=0, keepdims=True) for name in names]
    values = gates[...].astype(F32)
    slots = iota((512, 128), 0).astype(F32)
    table = jnp.zeros((512, 128), F32)
    for k in (0, 1):
        target = ids[k:k + 1, :].astype(F32) * 16.0 + ranks[k]
        table = table + jnp.where(slots == target, values[k:k + 1, :], 0.0)
    source = iota((128, 128), 0)
    order = pick(iota((128, 128), 1) == (source & 3) * 32 + (source >> 2)).astype(BF)
    v.pg[...] = dot(table.astype(BF), order, NN).astype(BF)
    row = iota((192, 256), 0)
    v.sel[...] = pick(iota((192, 256), 1) == row + 4 * twelfth(row)).astype(BF)
    block = twelfth(iota((16, 192), 1))
    sums = pick(iota((16, 192), 0) == block).astype(BF)
    tall = iota((192, 128), 0)
    mask = pick(iota((192, 128), 1) == tall - 12 * twelfth(tall))
    last = pick(iota((512, 32), 0) == iota((512, 32), 1) * 16 + 12).astype(BF)
    last_half = pick(iota((256, 16), 0) == iota((256, 16), 1) * 16 + 12).astype(BF)

    inputs = DepthGather(v.xv, 0, 384, v.xv_s.at[0], v.xv_r, me)

    def early(step, h):
        part = rows(384 * wrap(z + step) + 192 * h, 192)
        value, grade = gelu_pair(dot(v.xv[part, :], v.wi[...], NN))
        v.hid[part, :] = value.astype(BF)
        v.slope[part, :] = grade

    def product(h):
        def tile(t):
            return dot(v.buf[h * 512 + t * 256:h * 512 + t * 256 + 256, :], v.mwb[...], NT)

        @pl.when(c != h)
        def _():
            for t in (0, 1):
                v.sib_out[256 * t:256 * t + 256, :] = tile(t).astype(BF)
            send(v.sib_out, v.sib_in, v.sib_s.at[2], v.sib_r.at[2], other)

        @pl.when(c == h)
        def _():
            own = [tile(t) for t in (0, 1)]
            wait(v.sib_in, v.sib_r.at[2])
            for t in (0, 1):
                part = slice(256 * t, 256 * t + 256)
                v.tgc[part, :] = (own[t] + v.sib_in[part, :].astype(F32)).astype(BF)
            tokens.start()

    tokens = ChipSwap(
        lambda to: v.tgc.at[rows(32 * to, 32)],
        lambda k: v.tgs.at[rows(32 * lax.div(k, 4), 32), lanes(256 * lax.rem(k, 4), 256)],
        v.tgc, v.tk_s.at[0], v.tk_r.at[0], me,
    )
    there = [Dispatch(v.outb, v.inb.at[h], v.to_s.at[0], v.to_r.at[h], me) for h in (0, 1)]
    spread = [DepthGather(v.sc, 192 * h, 192, v.sc_s.at[h], v.sc_r.at[h], me) for h in (0, 1)]

    def dispatch(h):
        @pl.when(c == h)
        def _():
            tokens.arrive()
            for t in (0, 1):
                part = slice(512 * t, 512 * t + 512)
                v.outb[:, part] = dot(v.pg[...], v.tgs[:, part], NN).astype(BF)
            there[h].start()

    def to_experts(h):
        there[h].arrive()
        part = rows(384 * z + 192 * h, 192)
        v.sc[part, :] = dot(v.sel[...], v.inb[h], NN).astype(BF)
        spread[h].start()

    def chunk(h, step):
        q = wrap(z + step)
        part = rows(384 * q + 192 * h, 192)
        grad = dot(v.sc[part, :], v.wo[...], NT)
        column = jnp.sum(grad * v.hid[part, :].astype(F32), axis=1, keepdims=True)
        v.sgo[h, q] = dot(sums, (column * mask).astype(BF), NN).astype(BF)
        v.bg[part, :] = (grad * v.slope[part, :]).astype(BF)
        if step:
            send(v.sgo.at[h, q], v.sgi.at[h, z], v.sg_s.at[h], v.sg_r.at[h],
                 at(q, x, y, c))
        v.rp[part, :] = dot(v.bg[part, :], v.wi[...], NT).astype(BF)

    columns = ChipSwap(
        lambda to: merged.at[:, lanes(256 * to, 256)],
        lambda k: v.mc.at[rows(c * 512 + k * 32, 32)],
        v.mc, v.mc_s.at[0], v.mc_r.at[0], me,
    )
    head_weights = Fourfold(
        hw, lambda i, j: v.hwv.at[rows(1024 * i, 1024), lanes(128 * j, 128)], v.hwv,
        v.hw_s, v.hw_r.at[0], me,
    )
    waves, more = [half.steps() for half in gather]
    next(waves)
    inputs.start()
    send(li.at[:, other_half], v.liv.at[mine], v.sib_s.at[1], v.sib_r.at[1], other)
    next(waves)
    gather[1].first()
    wi_load.wait()
    early(0, 0)
    next(waves)
    early(0, 1)
    next(waves)
    next(waves)
    next(more)
    gather[0].finish()
    weights.arrive()
    product(0)
    next(more)
    next(more)
    dispatch(0)
    inputs.take()
    head_weights.start()
    next(more)
    next(more)
    gather[1].finish()
    product(1)
    to_experts(0)
    early(1, 0)
    early(3, 0)
    dispatch(1)
    inputs.finish()
    early(2, 0)
    wo_load.wait()
    chunk(0, 0)
    to_experts(1)
    columns.start()
    spread[0].take()
    li_load.wait()
    wait(v.liv.at[theirs], v.sib_r.at[1])
    gather_li[0].first()
    li_waves = [half.steps() for half in gather_li]
    chunk(0, 1)
    chunk(0, 3)
    next(li_waves[0])
    early(1, 1)
    spread[0].finish()
    chunk(0, 2)
    back = [
        DepthScatter(v.rp, 192 * h, 192, v.fb.at[h], v.wb.at[h], v.rp_s.at[h], v.rp_r.at[h], me)
        for h in (0, 1)
    ]
    back[0].open()
    early(3, 1)
    early(2, 1)
    spread[1].take()
    next(li_waves[0])
    chunk(1, 0)
    back[0].middle()
    chunk(1, 1)
    chunk(1, 3)
    next(li_waves[0])
    spread[1].finish()
    chunk(1, 2)
    back[1].open()
    for _ in li_waves[0]:
        pass
    gather_li[1].first()
    gather_li[0].finish()
    columns.arrive()
    mc_half = v.mc.at[rows(c * 512, 512)]
    send(mc_half, mc_half, v.sib_s.at[3], v.sib_r.at[3], other)

    def weight(t, _):
        part = lanes(256 * t, 256)
        down = rows(256 * t, 256)
        v.ingv[down, :] = dot(v.xv[:, part], v.bg[...], TN).astype(BF)
        v.outgv[down, :] = dot(v.hid[:, part], v.sc[...], TN).astype(BF)
        pltpu.make_async_copy(v.ingv.at[down], ing.at[down], v.out.at[0]).start()
        pltpu.make_async_copy(v.outgv.at[down], outg.at[down], v.out.at[1]).start()
        return 0

    def marks(h):
        wait(v.sgi.at[h, 0:3], v.sg_r.at[h])
        total = v.sgo[h, z].astype(F32)
        for step in (1, 2, 3):
            total = total + v.sgi[h, wrap(z + step)].astype(F32)
        return dot(last_half, total.astype(BF), NN)

    home = [
        Return(v.back.at[h], v.ret, h, v.fr_s.at[h], v.fr_r.at[0], me) for h in (0, 1)
    ]

    def from_experts(h):
        v.back[h] = dot(v.sel[...], back[h].total(), TN).astype(BF)
        v.back[h, :, 0:128] = (v.back[h, :, 0:128].astype(F32) + marks(h)).astype(BF)
        home[h].start()

    hog_columns = ChipSwap(
        lambda to: v.hogs.at[rows(32 * lax.div(to, 4), 32), lanes(256 * lax.rem(to, 4), 256)],
        lambda k: v.hc.at[rows(c * 512 + k * 32, 32)],
        v.hc, v.hc_s.at[0], v.hc_r.at[0], me,
    )
    hc_half = v.hc.at[rows(c * 512, 512)]

    def to_tokens(h):
        @pl.when(c == h)
        def _():
            home[h].arrive()
            for t in (0, 1):
                part = slice(512 * t, 512 * t + 512)
                v.hogs[:, part] = dot(v.pg[...], v.ret[:, part], TN).astype(BF)
            hog_columns.start()

    def to_columns(h):
        @pl.when(c == h)
        def _():
            hog_columns.arrive()
            send(hc_half, hc_half, v.sib_s.at[4], v.sib_r.at[4], other)

        @pl.when(c != h)
        def _():
            wait(v.hc.at[h * 512:h * 512 + 512], v.sib_r.at[4])

    lax.fori_loop(0, 1, weight, 0)
    back[1].middle()
    next(li_waves[1])
    lax.fori_loop(1, 2, weight, 0)
    from_experts(0)
    next(li_waves[1])
    lax.fori_loop(2, 4, weight, 0)
    next(li_waves[1])
    to_tokens(0)
    for _ in li_waves[1]:
        pass
    from_experts(1)
    wait(v.mc.at[rows((1 - c) * 512, 512)], v.sib_r.at[3])
    merge_sum = Fold(v.mgo, v.mgi, v.mg_s.at[0], v.mg_r.at[0], me)
    for tile in range(4):
        total = dot(v.mc[...], v.buf[:, tile * 512:tile * 512 + 512], TN).astype(BF)
        for j in (0, 1):
            v.mgo[(tile // 2) * 2 + j, :, (tile % 2) * 512:(tile % 2) * 512 + 512] = total[
                128 * j:128 * j + 128
            ]
    for half in gather:
        half.done()
    head_weights.arrive()

    def product_out(h):
        def tile(t, _):
            part = rows(h * 512 + 128 * t, 128)
            v.buf[part, :] = dot(v.hc[part, :], v.hwv[...], NT).astype(BF)
            return 0

        lax.fori_loop(0, 4, tile, 0)

    scatter = [
        PlaneScatter(v.buf, 512 * h, v.halves.at[h], v.wholes.at[h], v.ig_s.at[h], v.ig_r.at[h], me)
        for h in (0, 1)
    ]
    to_columns(0)
    product_out(0)
    scatter[0].first()
    for i in (0, 1):
        for j in (0, 1):
            merge_sum.start(i, j)
    adds = scatter[0].steps()
    next(adds)
    to_tokens(1)
    next(adds)
    to_columns(1)
    product_out(1)
    scatter[1].first()
    gather_li[1].finish()
    head_sum = Fold(v.hgo, v.hgi, v.hg_s.at[0], v.hg_r.at[0], me)
    for i in (0, 1):
        for tile in (0, 1):
            at_lane = i * 1024 + tile * 512
            total = dot(v.liv[:, at_lane:at_lane + 512], v.hc[...], TN)
            for j in (0, 1):
                v.hgo[i * 2 + j, tile * 512:tile * 512 + 512, :] = total[
                    :, 128 * j:128 * j + 128
                ].astype(BF)
        for j in (0, 1):
            head_sum.start(i, j)
    later = scatter[1].steps()
    next(adds)
    next(later)
    next(adds)

    def deliver(h):
        piece = v.buf.at[rows(h * 512 + chip * 32, 32)]

        @pl.when(c == h)
        def _():
            pltpu.make_async_copy(piece, ig.at[:, own_half], v.local.at[5]).start()

        @pl.when(c != h)
        def _():
            send(piece, ig.at[:, own_half], v.sib_s.at[5], v.sib_r.at[5], other)

    deliver(0)
    next(later)
    merge_sum.arrive()
    mg[...] = (v.mgi[0].astype(F32) + v.mgi[1].astype(F32)) + (
        v.mgi[2].astype(F32) + v.mgi[3].astype(F32)
    )
    next(later)
    found = dot(last, v.ret[:, 0:128], TN).astype(BF)
    for k in (0, 1):
        value = dot(found, names[k].astype(BF), TN)
        value = jnp.where(iota((128, 128), 0).astype(F32) == ranks[k], value, 0.0)
        gg[k:k + 1, :] = jnp.sum(value, axis=0, keepdims=True) / values[k:k + 1, :]
    next(later)
    deliver(1)
    head_sum.arrive()
    hg[...] = (v.hgi[0].astype(F32) + v.hgi[1].astype(F32)) + (
        v.hgi[2].astype(F32) + v.hgi[3].astype(F32)
    )
    for part in (weights, columns, inputs, tokens, *spread, *back, *home, *gather_li,
                 head_weights, merge_sum, hog_columns, head_sum, *scatter):
        part.done()

    wait(v.outb.at[0:496], v.to_s.at[0])
    for h in (0, 1):
        wait(v.sgo.at[h, 0:3], v.sg_s.at[h])
    wait(ing, v.out.at[0])
    wait(outg, v.out.at[1])
    for k, ref in enumerate((v.buf.at[mine], v.liv.at[mine], v.sib_out, mc_half, hc_half)):
        wait(ref, v.sib_s.at[k])
    wait(ig.at[:, own_half], v.local.at[5])
    wait(ig.at[:, other_half], v.sib_r.at[5])
    wait(v.buf.at[theirs], v.sib_s.at[5])


def widen_kernel(ig, hg, mg, ing, outg, to_ig, to_hg, to_mg, to_ing, to_outg,
                 narrow, wide, via_ig, via_hg, via_mg, s1, s2, s3, s4):
    through = ((ig, via_ig, to_ig), (hg, via_hg, to_hg), (mg, via_mg, to_mg))
    parts = [(src, dst, slice(256 * t, 256 * t + 256))
             for src, dst in ((ing, to_ing), (outg, to_outg)) for t in range(4)]
    loads = [
        pltpu.make_async_copy(src.at[part], narrow.at[k], s1.at[k])
        for k, (src, _, part) in enumerate(parts)
    ]
    stores = [
        pltpu.make_async_copy(wide.at[k], dst.at[part], s2.at[k])
        for k, (_, dst, part) in enumerate(parts)
    ]
    ins = [pltpu.make_async_copy(src, via, s3.at[k]) for k, (src, via, _) in enumerate(through)]
    outs = [pltpu.make_async_copy(via, dst, s4.at[k]) for k, (_, via, dst) in enumerate(through)]
    for copy in loads + ins:
        copy.start()
    for k in range(8):
        loads[k].wait()
        wide[k] = narrow[k].astype(F32)
        stores[k].start()
    for k in range(3):
        ins[k].wait()
        outs[k].start()
    for copy in stores + outs:
        copy.wait()


VM = pl.BlockSpec(memory_space=pltpu.VMEM)
ANY = pl.BlockSpec(memory_space=pl.ANY)


def body(
    layer_input, out_grad, merged, head_weight, merge_weight,
    expert_in, expert_out, dispatched, expert_ids, gate_values,
):
    outs = (
        ((32, 4096), BF), ((1024, 128), F32), ((128, 1024), F32),
        ((1024, 1024), BF), ((1024, 1024), BF), ((2, 128), F32),
    )
    *results, gate_grad = pl.pallas_call(
        kernel,
        out_shape=[jax.ShapeDtypeStruct(shape, kind) for shape, kind in outs],
        in_specs=[ANY] * 8 + [VM] * 2,
        out_specs=[ANY, VM, VM, ANY, ANY, VM],
        scratch_shapes=[pltpu.VMEM(*kind) for kind in SCRATCH.values()]
        + [dma(*shape) for shape in SEMS.values()],
        compiler_params=pltpu.CompilerParams(
            has_side_effects=True, collective_id=0, vmem_limit_bytes=LIMIT
        ),
        cost_estimate=pl.CostEstimate(flops=1 << 35, bytes_accessed=1 << 25, transcendentals=0),
    )(
        out_grad, merge_weight, merged, dispatched[0], expert_in[0], expert_out[0],
        layer_input, head_weight, expert_ids.T, gate_values.T,
    )
    input_total, head_grad, merge_grad, in_grad, out_weight_grad = pl.pallas_call(
        widen_kernel,
        out_shape=[
            jax.ShapeDtypeStruct(shape, kind)
            for shape, kind in (*outs[:3], ((1024, 1024), F32), ((1024, 1024), F32))
        ],
        in_specs=[ANY] * 5,
        out_specs=[ANY] * 5,
        scratch_shapes=[
            pltpu.VMEM((8, 256, 1024), BF), pltpu.VMEM((8, 256, 1024), F32),
            *[pltpu.VMEM(*kind) for kind in outs[:3]], dma(8), dma(8), dma(3), dma(3),
        ],
        compiler_params=pltpu.CompilerParams(vmem_limit_bytes=LIMIT),
        cost_estimate=pl.CostEstimate(flops=1 << 21, bytes_accessed=1 << 24, transcendentals=0),
    )(*results)
    return (
        input_total,
        head_grad,
        merge_grad,
        in_grad[None],
        out_weight_grad[None],
        gate_grad.T.astype(BF),
    )


def solution(mesh):
    placed = (
        P(("group", "expert"), None),
        P(("group", "expert"), None),
        P(("group", "expert"), None),
        P("group", "expert"),
        P("expert", "group"),
        P("expert", None, "group"),
        P("expert", "group", None),
        P("expert", "group", None),
        P(("group", "expert"), None),
        P(("group", "expert"), None),
    )
    return jax.shard_map(
        body,
        mesh=mesh,
        in_specs=placed,
        out_specs=(
            P(("group", "expert"), None),
            P("group", "expert"),
            P("expert", "group"),
            P("expert", None, "group"),
            P("expert", "group", None),
            P(("group", "expert"), None),
        ),
        check_vma=False,
    )
```

```python
import jax
import jax.numpy as jnp
from jax import lax
from jax.experimental import pallas as pl
from jax.experimental.pallas import tpu as pltpu
from jax.sharding import PartitionSpec as P

MESH = pl.DeviceIdType.MESH
BF = jnp.bfloat16
F32 = jnp.float32
LIMIT = 63 << 20

root_scale = 0.7978845608028654
cubic_term = 0.044715


def gelu_pair(value):
    square = value * value
    tangent = jnp.tanh(root_scale * value * (1.0 + cubic_term * square))
    half = 0.5 * (1.0 + tangent)
    slope = half + 0.5 * value * (1.0 - tangent * tangent) * root_scale * (
        1.0 + 3.0 * cubic_term * square
    )
    return value * half, slope


def dot(left, right, dims):
    return lax.dot_general(left, right, ((dims[:1], dims[1:]), ((), ())), preferred_element_type=F32)


NN, NT, TN = (1, 0), (1, 1), (0, 0)


def wrap(value):
    return lax.rem(value + 8, 4)


def place():
    e = lax.axis_index("expert")
    return lax.axis_index("group"), lax.rem(lax.div(e, 2), 4), lax.div(e, 8), lax.rem(e, 2)


def at(z, x, y, c):
    return {"group": z, "expert": (y * 4 + x) * 2 + c}


def by_chip(z, chip, c):
    return {"group": z, "expert": chip * 2 + c}


def rows(start, size):
    return pl.ds(pl.multiple_of(start, 16), size)


def lanes(start, size):
    return pl.ds(pl.multiple_of(start, 128), size)


def send(src, dst, ss, rs, device):
    pltpu.make_async_remote_copy(
        src_ref=src, dst_ref=dst, send_sem=ss, recv_sem=rs, device_id=device, device_id_type=MESH
    ).start()


def wait(ref, sem):
    pltpu.make_async_copy(ref, ref, sem).wait()


class PlaneGather:
    def __init__(self, buf, base, ss, rs, me):
        self.buf, self.base, self.ss, self.rs, self.me = buf, base, ss, rs, me

    def shift(self, h, i, j):
        z, x, y, c = self.me
        dx, dy = (i, j) if h == 0 else (j, i)
        return wrap(x + dx), wrap(y + dy)

    def piece(self, h, spot, half=None):
        px, py = self.shift(h, *spot)
        row = self.base + (py * 4 + px) * 32 + h * 16
        if half is None:
            return self.buf.at[rows(row, 16)]
        return self.buf.at[rows(row, 16), half * 1024:half * 1024 + 1024]

    def spot(self, stage, i, j):
        return (j, 0) if stage == 0 else (i, j)

    def ring(self, h, stage, i):
        return h * 5 + (0 if stage == 0 else 1 + i % 4)

    def sem(self, h, stage, i, kind):
        return self.rs.at[self.ring(h, stage, i) * 3 + min(kind, 2)]

    def post(self, ref, dst, h, stage, i, kind, step):
        px, py = self.shift(h, *((step, 0) if stage == 0 else (0, step)))
        send(ref, dst, self.ss, self.sem(h, stage, i, kind), at(self.me[0], px, py, self.me[3]))

    def begin(self, h, stage, i=0):
        ref = self.piece(h, self.spot(stage, i, 0))
        self.post(ref, ref, h, stage, i, 0, 1)
        self.post(ref, ref, h, stage, i, 1, -1)

    def take(self, h, stage, i, kind):
        spot = self.spot(stage, i, (-1, 1)[kind])
        wait(self.piece(h, spot), self.sem(h, stage, i, kind))
        ref = self.piece(h, spot, kind)
        self.post(ref, ref, h, stage, i, kind + 2, (1, -1)[kind])

    def relay(self, h, stage, i=0):
        self.take(h, stage, i, 0)
        self.take(h, stage, i, 1)

    def close(self, h, stage, i=0):
        wait(self.piece(h, self.spot(stage, i, 2)), self.sem(h, stage, i, 2))

    def first(self):
        for h in (0, 1):
            self.begin(h, 0)
            self.begin(h, 1, 0)

    def steps(self):
        for h in (0, 1):
            self.take(h, 0, 0, 0)
            self.begin(h, 1, -1)
            self.take(h, 0, 0, 1)
            self.begin(h, 1, 1)
        yield
        for h in (0, 1):
            self.relay(h, 1, 0)
        for h in (0, 1):
            self.close(h, 0)
            self.begin(h, 1, 2)
        yield
        for i in (-1, 1):
            for h in (0, 1):
                self.relay(h, 1, i)
            yield
        for h in (0, 1):
            self.relay(h, 1, 2)
        yield

    def finish(self):
        for i in (0, -1, 1, 2):
            for h in (0, 1):
                self.close(h, 1, i)

    def done(self):
        wait(self.buf.at[self.base:self.base + 480], self.ss)


class PlaneScatter(PlaneGather):
    def __init__(self, buf, base, halves, wholes, ss, rs, me):
        super().__init__(buf, base, ss, rs, me)
        self.halves, self.wholes = halves, wholes

    def sem(self, h, stage, i, kind):
        return self.rs.at[self.ring(h, stage, i) * 2 + kind // 2]

    def open(self, h, stage, i=0):
        r = self.ring(h, stage, i)
        for kind, step in ((0, 1), (1, -1)):
            ref = self.piece(h, self.spot(stage, i, 2), kind)
            self.post(ref, self.halves.at[r, kind], h, stage, i, kind, step)

    def middle(self, h, stage, i=0):
        r = self.ring(h, stage, i)
        wait(self.halves.at[r], self.sem(h, stage, i, 0))
        for kind, step in ((0, 1), (1, -1)):
            got = self.halves.at[r, kind]
            own = self.piece(h, self.spot(stage, i, step), kind)
            own[...] = (own[...].astype(F32) + got[...].astype(F32)).astype(BF)
            ref = self.piece(h, self.spot(stage, i, step))
            self.post(ref, self.wholes.at[r, kind], h, stage, i, kind + 2, step)

    def add(self, h, stage, i=0):
        r = self.ring(h, stage, i)
        wait(self.wholes.at[r], self.sem(h, stage, i, 2))
        own = self.piece(h, self.spot(stage, i, 0))
        own[...] = (
            own[...].astype(F32)
            + self.wholes[r, 0].astype(F32)
            + self.wholes[r, 1].astype(F32)
        ).astype(BF)

    def first(self):
        for i in (2, -1, 1, 0):
            for h in (0, 1):
                self.open(h, 1, i)

    def steps(self):
        for i in (2, -1, 1, 0):
            for h in (0, 1):
                self.middle(h, 1, i)
        yield
        for h in (0, 1):
            self.add(h, 1, 2)
            self.open(h, 0)
        for i in (-1, 1):
            for h in (0, 1):
                self.add(h, 1, i)
        yield
        for h in (0, 1):
            self.middle(h, 0)
        for h in (0, 1):
            self.add(h, 1, 0)
        yield
        for h in (0, 1):
            self.add(h, 0)
        yield


class Fourfold:
    def __init__(self, src, slot, dst, ss, rs, me):
        self.src, self.slot, self.dst, self.ss, self.rs, self.me = src, slot, dst, ss, rs, me
        z, x, y, c = me
        self.core = lax.div(z, 2)
        self.own = self.core == c

    def start(self):
        z, x, y, c = self.me
        dst = self.slot(lax.rem(z, 2), c)
        @pl.when(self.own)
        def _():
            pltpu.make_async_copy(self.src, dst, self.rs).start()

        @pl.when(jnp.logical_not(self.own))
        def _():
            send(self.src, dst, self.ss.at[1], self.rs, at(z, x, y, self.core))

        for k in (1, 3, 2):
            send(self.src, dst, self.ss.at[0], self.rs, at(wrap(z + k), x, y, self.core))

    def arrive(self):
        wait(self.dst, self.rs)

    def done(self):
        @pl.when(jnp.logical_not(self.own))
        def _():
            wait(self.src, self.ss.at[1])

        wait(self.dst.at[0:self.dst.shape[0] * 3 // 4], self.ss.at[0])


class Fold:
    def __init__(self, out, got, ss, rs, me):
        self.out, self.got, self.ss, self.rs, self.me = out, got, ss, rs, me

    def start(self, i, j):
        z, x, y, c = self.me
        p = i * 2 + j
        to = 2 * c + i
        own = jnp.logical_and(to == z, c == j)

        @pl.when(own)
        def _():
            pltpu.make_async_copy(self.out.at[p], self.got.at[z], self.rs).start()

        @pl.when(jnp.logical_not(own))
        def _():
            send(self.out.at[p], self.got.at[z], self.ss, self.rs, at(to, x, y, j))

    def arrive(self):
        wait(self.got, self.rs)

    def done(self):
        z, x, y, c = self.me
        own = lax.div(z, 2) == c

        @pl.when(own)
        def _():
            wait(self.out.at[0:3], self.ss)

        @pl.when(jnp.logical_not(own))
        def _():
            wait(self.out, self.ss)


class ChipSwap:
    def __init__(self, src, dst, size, ss, rs, me):
        self.src, self.dst, self.size, self.ss, self.rs, self.me = src, dst, size, ss, rs, me
        self.chip = me[2] * 4 + me[1]

    def start(self):
        z, x, y, c = self.me
        mine = self.chip

        def step(k, _):
            to = lax.rem(mine + k, 16)
            send(self.src(to), self.dst(mine), self.ss, self.rs, by_chip(z, to, c))
            return 0

        pltpu.make_async_copy(self.src(mine), self.dst(mine), self.rs).start()
        lax.fori_loop(1, 16, step, 0)

    def arrive(self):
        wait(self.size.at[0:512], self.rs)

    def done(self):
        wait(self.size.at[0:480], self.ss)


class Dispatch:
    def __init__(self, out, got, ss, rs, me):
        self.out, self.got, self.ss, self.rs, self.me = out, got, ss, rs, me
        self.chip = me[2] * 4 + me[1]
        self.e = self.chip * 2 + me[3]

    def start(self):
        dst, sem = self.got.at[rows(16 * self.chip, 16)], self.rs

        def step(k, _):
            to = lax.rem(self.e + k, 32)
            send(self.out.at[rows(16 * to, 16)], dst, self.ss, sem,
                 {"group": self.me[0], "expert": to})
            return 0

        pltpu.make_async_copy(self.out.at[rows(16 * self.e, 16)], dst, sem).start()
        lax.fori_loop(1, 32, step, 0)

    def arrive(self):
        wait(self.got, self.rs)


class Return:
    def __init__(self, out, got, half, ss, rs, me):
        self.out, self.got, self.half, self.ss, self.rs, self.me = out, got, half, ss, rs, me
        self.chip = me[2] * 4 + me[1]
        self.e = self.chip * 2 + me[3]

    def start(self):
        dst, sem = self.got.at[rows(16 * self.e, 16)], self.rs

        def step(k, _):
            to = lax.rem(self.chip + k, 16)
            send(self.out.at[rows(16 * to, 16)], dst, self.ss.at[0], sem,
                 by_chip(self.me[0], to, self.half))
            return 0

        lax.fori_loop(1, 16, step, 0)
        own = self.out.at[rows(16 * self.chip, 16)]

        @pl.when(self.me[3] == self.half)
        def _():
            pltpu.make_async_copy(own, dst, sem).start()

        @pl.when(self.me[3] != self.half)
        def _():
            send(own, dst, self.ss.at[1], sem, by_chip(self.me[0], self.chip, self.half))

    def arrive(self):
        wait(self.got, self.rs)

    def done(self):
        wait(self.out.at[0:240], self.ss.at[0])

        @pl.when(self.me[3] != self.half)
        def _():
            wait(self.out.at[0:16], self.ss.at[1])


class DepthGather:
    def __init__(self, buf, base, size, ss, rs, me):
        self.buf, self.base, self.size, self.ss, self.rs, self.me = buf, base, size, ss, rs, me

    def piece(self, step, half=None):
        row = 384 * wrap(self.me[0] + step) + self.base
        if half is None:
            return self.buf.at[rows(row, self.size)]
        return self.buf.at[rows(row + self.size // 2 * half, self.size // 2)]

    def to(self, step):
        z, x, y, c = self.me
        return at(wrap(z + step), x, y, c)

    def start(self):
        own = self.piece(0)
        send(own, own, self.ss, self.rs.at[0], self.to(1))
        send(own, own, self.ss, self.rs.at[1], self.to(-1))

    def take(self):
        for kind, step in ((0, -1), (1, 1)):
            wait(self.piece(step), self.rs.at[kind])
            half = self.piece(step, kind)
            send(half, half, self.ss, self.rs.at[2], self.to(-step))

    def finish(self):
        wait(self.piece(2), self.rs.at[2])

    def done(self):
        wait(self.buf.at[0:3 * self.size], self.ss)


class DepthScatter(DepthGather):
    def __init__(self, buf, base, size, halves, wholes, ss, rs, me):
        super().__init__(buf, base, size, ss, rs, me)
        self.halves, self.wholes = halves, wholes

    def open(self):
        for kind, step in ((0, 1), (1, -1)):
            send(self.piece(2, kind), self.halves.at[kind], self.ss, self.rs.at[0], self.to(step))

    def middle(self):
        wait(self.halves, self.rs.at[0])
        for kind, step in ((0, 1), (1, -1)):
            own = self.piece(step, kind)
            own[...] = (own[...].astype(F32) + self.halves[kind].astype(F32)).astype(BF)
            send(self.piece(step), self.wholes.at[kind], self.ss, self.rs.at[1], self.to(step))

    def total(self):
        wait(self.wholes, self.rs.at[1])
        return (
            self.piece(0)[...].astype(F32)
            + self.wholes[0].astype(F32)
            + self.wholes[1].astype(F32)
        ).astype(BF)


def dma(*shape):
    return pltpu.SemaphoreType.DMA(shape)


def iota(shape, dim):
    return lax.broadcasted_iota(jnp.int32, shape, dim)


def pick(condition):
    return jnp.where(condition, 1.0, 0.0)


def twelfth(value):
    return (value * 5462) >> 16


SCRATCH = dict(
    buf=((1024, 2048), BF), mwb=((256, 2048), BF), mc=((1024, 256), BF),
    sib_out=((512, 256), BF), sib_in=((512, 256), BF), tgc=((512, 256), BF), tgs=((128, 1024), BF),
    pg=((512, 128), BF), sel=((192, 256), BF),
    outb=((512, 1024), BF), inb=((2, 256, 1024), BF),
    sc=((1536, 1024), BF), xv=((1536, 1024), BF), wi=((1024, 1024), BF), wo=((1024, 1024), BF),
    hid=((1536, 1024), BF), slope=((1536, 1024), F32), bg=((1536, 1024), BF), rp=((1536, 1024), BF),
    fb=((2, 2, 96, 1024), BF), wb=((2, 2, 192, 1024), BF),
    sgo=((2, 4, 16, 128), BF), sgi=((2, 4, 16, 128), BF),
    back=((2, 256, 1024), BF), ret=((512, 1024), BF),
    hogs=((128, 1024), BF), hc=((1024, 256), BF), liv=((1024, 2048), BF), hwv=((2048, 256), BF),
    halves=((2, 10, 2, 16, 1024), BF), wholes=((2, 10, 2, 16, 2048), BF),
    hgo=((4, 1024, 128), BF), hgi=((4, 1024, 128), BF),
    mgo=((4, 128, 1024), BF), mgi=((4, 128, 1024), BF),
    ingv=((1024, 1024), BF), outgv=((1024, 1024), BF),
)
SEMS = dict(
    og_s=(2,), og_r=(2, 30), li_s=(2,), li_r=(2, 30), ig_s=(2,), ig_r=(2, 20),
    mw_s=(2,), mw_r=(1,), hw_s=(2,), hw_r=(1,),
    mc_s=(1,), mc_r=(1,), tk_s=(1,), tk_r=(1,), hc_s=(1,), hc_r=(1,),
    to_s=(1,), to_r=(2,), fr_s=(2, 2), fr_r=(1,),
    xv_s=(1,), xv_r=(3,), sc_s=(2,), sc_r=(2, 3), rp_s=(2,), rp_r=(2, 2),
    sg_s=(2,), sg_r=(2,), mg_s=(1,), mg_r=(1,), hg_s=(1,), hg_r=(1,),
    local=(6,), out=(2,), sib_s=(6,), sib_r=(6,),
)
NAMES = list(SCRATCH) + list(SEMS)


class Named:
    def __init__(self, names, refs):
        for name, ref in zip(names, refs, strict=True):
            setattr(self, name, ref)


def kernel(og, mw, merged, disp, w_in, w_out, li, hw, ids, gates,
           ig, hg, mg, ing, outg, gg, *refs):
    v = Named(NAMES, refs)
    me = place()
    z, x, y, c = me
    chip = y * 4 + x
    e = chip * 2 + c
    other = at(z, x, y, 1 - c)

    barrier = pltpu.get_barrier_semaphore()

    def greet(k, _):
        pl.semaphore_signal(
            barrier, inc=1, device_id={"group": z, "expert": lax.rem(e + k, 32)},
            device_id_type=MESH,
        )
        return 0

    lax.fori_loop(1, 32, greet, 0)
    for step in (1, 2, 3):
        for core in (0, 1):
            pl.semaphore_signal(
                barrier, inc=1, device_id=at(wrap(z + step), x, y, core), device_id_type=MESH
            )

    def local(src, dst, k):
        copy = pltpu.make_async_copy(src, dst, v.local.at[k])
        copy.start()
        return copy

    mine = rows(c * 512 + chip * 32, 32)
    theirs = rows((1 - c) * 512 + chip * 32, 32)
    own_half, other_half = lanes(c * 2048, 2048), lanes((1 - c) * 2048, 2048)
    own_rows = rows(384 * z, 384)
    raw = v.rp.at[0:384]
    xv_load = local(disp, raw, 1)
    og_load = local(og.at[:, own_half], v.buf.at[mine], 0)
    wi_load = local(w_in, v.wi, 3)
    li_load = local(li.at[:, own_half], v.liv.at[mine], 2)
    wo_load = local(w_out, v.wo, 4)

    row = iota((384, 384), 0)
    late = (row >= 192).astype(jnp.int32)
    first = row - 192 * late
    order = pick(iota((384, 384), 1) == first + 12 * twelfth(first) + 12 * late).astype(BF)
    xv_load.wait()
    v.xv[own_rows, :] = dot(order, raw[...], NN).astype(BF)
    pl.semaphore_wait(barrier, 37)

    send(og.at[:, other_half], v.buf.at[mine], v.sib_s.at[0], v.sib_r.at[0], other)
    weights = Fourfold(
        mw, lambda i, j: v.mwb.at[rows(128 * j, 128), lanes(1024 * i, 1024)], v.mwb,
        v.mw_s, v.mw_r.at[0], me,
    )
    weights.start()
    gather = [PlaneGather(v.buf, 512 * h, v.og_s.at[h], v.og_r.at[h], me) for h in (0, 1)]
    gather_li = [PlaneGather(v.liv, 512 * h, v.li_s.at[h], v.li_r.at[h], me) for h in (0, 1)]
    og_load.wait()
    wait(v.buf.at[theirs], v.sib_r.at[0])
    gather[0].first()

    names = [pick(iota((32, 128), 0) == ids[k:k + 1, :]) for k in (0, 1)]
    before = pick(iota((128, 128), 0) < iota((128, 128), 1)).astype(BF)
    counts = dot((names[0] + names[1]).astype(BF), before, NN)
    ranks = [jnp.sum(name * counts, axis=0, keepdims=True) for name in names]
    values = gates[...].astype(F32)
    slots = iota((512, 128), 0).astype(F32)
    table = jnp.zeros((512, 128), F32)
    for k in (0, 1):
        target = ids[k:k + 1, :].astype(F32) * 16.0 + ranks[k]
        table = table + jnp.where(slots == target, values[k:k + 1, :], 0.0)
    source = iota((128, 128), 0)
    order = pick(iota((128, 128), 1) == (source & 3) * 32 + (source >> 2)).astype(BF)
    v.pg[...] = dot(table.astype(BF), order, NN).astype(BF)
    row = iota((192, 256), 0)
    v.sel[...] = pick(iota((192, 256), 1) == row + 4 * twelfth(row)).astype(BF)
    block = twelfth(iota((16, 192), 1))
    sums = pick(iota((16, 192), 0) == block).astype(BF)
    tall = iota((192, 128), 0)
    mask = pick(iota((192, 128), 1) == tall - 12 * twelfth(tall))
    last = pick(iota((512, 32), 0) == iota((512, 32), 1) * 16 + 12).astype(BF)
    last_half = pick(iota((256, 16), 0) == iota((256, 16), 1) * 16 + 12).astype(BF)

    inputs = DepthGather(v.xv, 0, 384, v.xv_s.at[0], v.xv_r, me)

    def early(step, h):
        part = rows(384 * wrap(z + step) + 192 * h, 192)
        value, grade = gelu_pair(dot(v.xv[part, :], v.wi[...], NN))
        v.hid[part, :] = value.astype(BF)
        v.slope[part, :] = grade

    def product(h):
        def tile(t):
            return dot(v.buf[h * 512 + t * 256:h * 512 + t * 256 + 256, :], v.mwb[...], NT)

        @pl.when(c != h)
        def _():
            for t in (0, 1):
                v.sib_out[256 * t:256 * t + 256, :] = tile(t).astype(BF)
            send(v.sib_out, v.sib_in, v.sib_s.at[2], v.sib_r.at[2], other)

        @pl.when(c == h)
        def _():
            own = [tile(t) for t in (0, 1)]
            wait(v.sib_in, v.sib_r.at[2])
            for t in (0, 1):
                part = slice(256 * t, 256 * t + 256)
                v.tgc[part, :] = (own[t] + v.sib_in[part, :].astype(F32)).astype(BF)
            tokens.start()

    tokens = ChipSwap(
        lambda to: v.tgc.at[rows(32 * to, 32)],
        lambda k: v.tgs.at[rows(32 * lax.div(k, 4), 32), lanes(256 * lax.rem(k, 4), 256)],
        v.tgc, v.tk_s.at[0], v.tk_r.at[0], me,
    )
    there = [Dispatch(v.outb, v.inb.at[h], v.to_s.at[0], v.to_r.at[h], me) for h in (0, 1)]
    spread = [DepthGather(v.sc, 192 * h, 192, v.sc_s.at[h], v.sc_r.at[h], me) for h in (0, 1)]

    def dispatch(h):
        @pl.when(c == h)
        def _():
            tokens.arrive()
            for t in (0, 1):
                part = slice(512 * t, 512 * t + 512)
                v.outb[:, part] = dot(v.pg[...], v.tgs[:, part], NN).astype(BF)
            there[h].start()

    def to_experts(h):
        there[h].arrive()
        part = rows(384 * z + 192 * h, 192)
        v.sc[part, :] = dot(v.sel[...], v.inb[h], NN).astype(BF)
        spread[h].start()

    def chunk(h, step):
        q = wrap(z + step)
        part = rows(384 * q + 192 * h, 192)
        grad = dot(v.sc[part, :], v.wo[...], NT)
        column = jnp.sum(grad * v.hid[part, :].astype(F32), axis=1, keepdims=True)
        v.sgo[h, q] = dot(sums, (column * mask).astype(BF), NN).astype(BF)
        v.bg[part, :] = (grad * v.slope[part, :]).astype(BF)
        if step:
            send(v.sgo.at[h, q], v.sgi.at[h, z], v.sg_s.at[h], v.sg_r.at[h],
                 at(q, x, y, c))
        v.rp[part, :] = dot(v.bg[part, :], v.wi[...], NT).astype(BF)

    columns = ChipSwap(
        lambda to: merged.at[:, lanes(256 * to, 256)],
        lambda k: v.mc.at[rows(c * 512 + k * 32, 32)],
        v.mc, v.mc_s.at[0], v.mc_r.at[0], me,
    )
    head_weights = Fourfold(
        hw, lambda i, j: v.hwv.at[rows(1024 * i, 1024), lanes(128 * j, 128)], v.hwv,
        v.hw_s, v.hw_r.at[0], me,
    )
    waves, more = [half.steps() for half in gather]
    next(waves)
    inputs.start()
    send(li.at[:, other_half], v.liv.at[mine], v.sib_s.at[1], v.sib_r.at[1], other)
    next(waves)
    gather[1].first()
    wi_load.wait()
    early(0, 0)
    next(waves)
    early(0, 1)
    next(waves)
    next(waves)
    next(more)
    gather[0].finish()
    weights.arrive()
    head_weights.start()
    product(0)
    next(more)
    next(more)
    dispatch(0)
    inputs.take()
    next(more)
    next(more)
    gather[1].finish()
    product(1)
    to_experts(0)
    early(1, 0)
    early(3, 0)
    dispatch(1)
    inputs.finish()
    early(2, 0)
    wo_load.wait()
    chunk(0, 0)
    to_experts(1)
    columns.start()
    spread[0].take()
    li_load.wait()
    wait(v.liv.at[theirs], v.sib_r.at[1])
    gather_li[0].first()
    gather_li[1].first()
    li_waves = [half.steps() for half in gather_li]
    chunk(0, 1)
    chunk(0, 3)
    next(li_waves[0])
    early(1, 1)
    spread[0].finish()
    chunk(0, 2)
    back = [
        DepthScatter(v.rp, 192 * h, 192, v.fb.at[h], v.wb.at[h], v.rp_s.at[h], v.rp_r.at[h], me)
        for h in (0, 1)
    ]
    back[0].open()
    early(3, 1)
    early(2, 1)
    spread[1].take()
    next(li_waves[0])
    chunk(1, 0)
    back[0].middle()
    chunk(1, 1)
    chunk(1, 3)
    next(li_waves[0])
    spread[1].finish()
    chunk(1, 2)
    back[1].open()
    for _ in li_waves[0]:
        pass
    gather_li[0].finish()
    columns.arrive()
    mc_half = v.mc.at[rows(c * 512, 512)]
    send(mc_half, mc_half, v.sib_s.at[3], v.sib_r.at[3], other)

    def weight(t, _):
        part = lanes(256 * t, 256)
        down = rows(256 * t, 256)
        v.ingv[down, :] = dot(v.xv[:, part], v.bg[...], TN).astype(BF)
        v.outgv[down, :] = dot(v.hid[:, part], v.sc[...], TN).astype(BF)
        pltpu.make_async_copy(v.ingv.at[down], ing.at[down], v.out.at[0]).start()
        pltpu.make_async_copy(v.outgv.at[down], outg.at[down], v.out.at[1]).start()
        return 0

    def marks(h):
        wait(v.sgi.at[h, 0:3], v.sg_r.at[h])
        total = v.sgo[h, z].astype(F32)
        for step in (1, 2, 3):
            total = total + v.sgi[h, wrap(z + step)].astype(F32)
        return dot(last_half, total.astype(BF), NN)

    home = [
        Return(v.back.at[h], v.ret, h, v.fr_s.at[h], v.fr_r.at[0], me) for h in (0, 1)
    ]

    def from_experts(h):
        v.back[h] = dot(v.sel[...], back[h].total(), TN).astype(BF)
        v.back[h, :, 0:128] = (v.back[h, :, 0:128].astype(F32) + marks(h)).astype(BF)
        home[h].start()

    hog_columns = ChipSwap(
        lambda to: v.hogs.at[rows(32 * lax.div(to, 4), 32), lanes(256 * lax.rem(to, 4), 256)],
        lambda k: v.hc.at[rows(c * 512 + k * 32, 32)],
        v.hc, v.hc_s.at[0], v.hc_r.at[0], me,
    )
    hc_half = v.hc.at[rows(c * 512, 512)]

    def to_tokens(h):
        @pl.when(c == h)
        def _():
            home[h].arrive()
            for t in (0, 1):
                part = slice(512 * t, 512 * t + 512)
                v.hogs[:, part] = dot(v.pg[...], v.ret[:, part], TN).astype(BF)
            hog_columns.start()

    def to_columns(h):
        @pl.when(c == h)
        def _():
            hog_columns.arrive()
            send(hc_half, hc_half, v.sib_s.at[4], v.sib_r.at[4], other)

        @pl.when(c != h)
        def _():
            wait(v.hc.at[h * 512:h * 512 + 512], v.sib_r.at[4])

    lax.fori_loop(0, 1, weight, 0)
    back[1].middle()
    next(li_waves[1])
    lax.fori_loop(1, 2, weight, 0)
    from_experts(0)
    next(li_waves[1])
    lax.fori_loop(2, 4, weight, 0)
    next(li_waves[1])
    to_tokens(0)
    for _ in li_waves[1]:
        pass
    from_experts(1)
    wait(v.mc.at[rows((1 - c) * 512, 512)], v.sib_r.at[3])
    merge_sum = Fold(v.mgo, v.mgi, v.mg_s.at[0], v.mg_r.at[0], me)
    for tile in range(4):
        total = dot(v.mc[...], v.buf[:, tile * 512:tile * 512 + 512], TN).astype(BF)
        for j in (0, 1):
            v.mgo[(tile // 2) * 2 + j, :, (tile % 2) * 512:(tile % 2) * 512 + 512] = total[
                128 * j:128 * j + 128
            ]
    for half in gather:
        half.done()
    head_weights.arrive()

    def product_out(h):
        def tile(t, _):
            part = rows(h * 512 + 128 * t, 128)
            v.buf[part, :] = dot(v.hc[part, :], v.hwv[...], NT).astype(BF)
            return 0

        lax.fori_loop(0, 4, tile, 0)

    scatter = [
        PlaneScatter(v.buf, 512 * h, v.halves.at[h], v.wholes.at[h], v.ig_s.at[h], v.ig_r.at[h], me)
        for h in (0, 1)
    ]
    to_columns(0)
    product_out(0)
    scatter[0].first()
    for i in (0, 1):
        for j in (0, 1):
            merge_sum.start(i, j)
    adds = scatter[0].steps()
    next(adds)
    to_tokens(1)
    next(adds)
    to_columns(1)
    product_out(1)
    scatter[1].first()
    gather_li[1].finish()
    head_sum = Fold(v.hgo, v.hgi, v.hg_s.at[0], v.hg_r.at[0], me)
    for i in (0, 1):
        for tile in (0, 1):
            at_lane = i * 1024 + tile * 512
            total = dot(v.liv[:, at_lane:at_lane + 512], v.hc[...], TN)
            for j in (0, 1):
                v.hgo[i * 2 + j, tile * 512:tile * 512 + 512, :] = total[
                    :, 128 * j:128 * j + 128
                ].astype(BF)
        for j in (0, 1):
            head_sum.start(i, j)
    later = scatter[1].steps()
    next(adds)
    next(later)
    next(adds)

    def deliver(h):
        piece = v.buf.at[rows(h * 512 + chip * 32, 32)]

        @pl.when(c == h)
        def _():
            pltpu.make_async_copy(piece, ig.at[:, own_half], v.local.at[5]).start()

        @pl.when(c != h)
        def _():
            send(piece, ig.at[:, own_half], v.sib_s.at[5], v.sib_r.at[5], other)

    deliver(0)
    next(later)
    merge_sum.arrive()
    mg[...] = (v.mgi[0].astype(F32) + v.mgi[1].astype(F32)) + (
        v.mgi[2].astype(F32) + v.mgi[3].astype(F32)
    )
    next(later)
    shares = []
    found = dot(last, v.ret[:, 0:128], TN).astype(BF)
    for k in (0, 1):
        value = dot(found, names[k].astype(BF), TN)
        value = jnp.where(iota((128, 128), 0).astype(F32) == ranks[k], value, 0.0)
        shares.append(jnp.sum(value, axis=0, keepdims=True) / values[k:k + 1, :])
    gg[...] = jnp.concatenate(shares, axis=0).astype(BF)
    next(later)
    deliver(1)
    head_sum.arrive()
    hg[...] = (v.hgi[0].astype(F32) + v.hgi[1].astype(F32)) + (
        v.hgi[2].astype(F32) + v.hgi[3].astype(F32)
    )
    for part in (weights, columns, inputs, tokens, *spread, *back, *home, *gather_li,
                 head_weights, merge_sum, hog_columns, head_sum, *scatter):
        part.done()

    wait(v.outb.at[0:496], v.to_s.at[0])
    for h in (0, 1):
        wait(v.sgo.at[h, 0:3], v.sg_s.at[h])
    wait(ing, v.out.at[0])
    wait(outg, v.out.at[1])
    for k, ref in enumerate((v.buf.at[mine], v.liv.at[mine], v.sib_out, mc_half, hc_half)):
        wait(ref, v.sib_s.at[k])
    wait(ig.at[:, own_half], v.local.at[5])
    wait(ig.at[:, other_half], v.sib_r.at[5])
    wait(v.buf.at[theirs], v.sib_s.at[5])


def widen_kernel(ig, hg, mg, ing, outg, to_ig, to_hg, to_mg, to_ing, to_outg,
                 narrow, wide, via_ig, via_hg, via_mg, s1, s2, s3, s4):
    through = ((ig, via_ig, to_ig), (hg, via_hg, to_hg), (mg, via_mg, to_mg))
    parts = [(src, dst, slice(256 * t, 256 * t + 256))
             for src, dst in ((ing, to_ing), (outg, to_outg)) for t in range(4)]
    loads = [
        pltpu.make_async_copy(src.at[part], narrow.at[k], s1.at[k])
        for k, (src, _, part) in enumerate(parts)
    ]
    stores = [
        pltpu.make_async_copy(wide.at[k], dst.at[part], s2.at[k])
        for k, (_, dst, part) in enumerate(parts)
    ]
    ins = [pltpu.make_async_copy(src, via, s3.at[k]) for k, (src, via, _) in enumerate(through)]
    outs = [pltpu.make_async_copy(via, dst, s4.at[k]) for k, (_, via, dst) in enumerate(through)]
    for copy in loads + ins:
        copy.start()
    for k in range(8):
        loads[k].wait()
        wide[k] = narrow[k].astype(F32)
        stores[k].start()
    for k in range(3):
        ins[k].wait()
        outs[k].start()
    for copy in stores + outs:
        copy.wait()


VM = pl.BlockSpec(memory_space=pltpu.VMEM)
ANY = pl.BlockSpec(memory_space=pl.ANY)


def body(
    layer_input, out_grad, merged, head_weight, merge_weight,
    expert_in, expert_out, dispatched, expert_ids, gate_values,
):
    outs = (
        ((32, 4096), BF), ((1024, 128), F32), ((128, 1024), F32),
        ((1024, 1024), BF), ((1024, 1024), BF), ((2, 128), BF),
    )
    *results, gate_grad = pl.pallas_call(
        kernel,
        out_shape=[jax.ShapeDtypeStruct(shape, kind) for shape, kind in outs],
        in_specs=[ANY] * 8 + [VM] * 2,
        out_specs=[ANY, VM, VM, ANY, ANY, VM],
        scratch_shapes=[pltpu.VMEM(*kind) for kind in SCRATCH.values()]
        + [dma(*shape) for shape in SEMS.values()],
        compiler_params=pltpu.CompilerParams(
            has_side_effects=True, collective_id=0, vmem_limit_bytes=LIMIT
        ),
        cost_estimate=pl.CostEstimate(flops=1 << 35, bytes_accessed=1 << 25, transcendentals=0),
    )(
        out_grad, merge_weight, merged, dispatched[0], expert_in[0], expert_out[0],
        layer_input, head_weight, expert_ids.T, gate_values.T,
    )
    input_total, head_grad, merge_grad, in_grad, out_weight_grad = pl.pallas_call(
        widen_kernel,
        out_shape=[
            jax.ShapeDtypeStruct(shape, kind)
            for shape, kind in (*outs[:3], ((1024, 1024), F32), ((1024, 1024), F32))
        ],
        in_specs=[ANY] * 5,
        out_specs=[ANY] * 5,
        scratch_shapes=[
            pltpu.VMEM((8, 256, 1024), BF), pltpu.VMEM((8, 256, 1024), F32),
            *[pltpu.VMEM(*kind) for kind in outs[:3]], dma(8), dma(8), dma(3), dma(3),
        ],
        compiler_params=pltpu.CompilerParams(vmem_limit_bytes=LIMIT),
        cost_estimate=pl.CostEstimate(flops=1 << 21, bytes_accessed=1 << 24, transcendentals=0),
    )(*results)
    return (
        input_total,
        head_grad,
        merge_grad,
        in_grad[None],
        out_weight_grad[None],
        gate_grad.T,
    )


def solution(mesh):
    placed = (
        P(("group", "expert"), None),
        P(("group", "expert"), None),
        P(("group", "expert"), None),
        P("group", "expert"),
        P("expert", "group"),
        P("expert", None, "group"),
        P("expert", "group", None),
        P("expert", "group", None),
        P(("group", "expert"), None),
        P(("group", "expert"), None),
    )
    return jax.shard_map(
        body,
        mesh=mesh,
        in_specs=placed,
        out_specs=(
            P(("group", "expert"), None),
            P("group", "expert"),
            P("expert", "group"),
            P("expert", None, "group"),
            P("expert", "group", None),
            P(("group", "expert"), None),
        ),
        check_vma=False,
    )
```
